256 devices in a mesh: dp: 64 (over z, x, core), pipe: 4 (over y).
Axes of the slice: x: 4, y: 4, z: 8, core: 2. Of those that a mesh axis runs over, the one named last changes fastest.
Arguments:
- perturbed: bfloat16 [2, 4096, 4096], P(None, 'dp'), may hold values from -6 to 6
- control_token_states: bfloat16 [2, 4096, 4096], P(None, 'dp'), may hold values from -6 to 6
- owners: int32 [2, 4096, 1], P(None, 'dp'), may hold values from 0 to 63; in each aligned block of 64 rows (0 to 63, 64 to 127, ..., all dimensions but the last counted through in order) at most 4 rows name the same one
- matched_control_row: int32 [2, 4096], P(None, 'dp'), may hold values from 0 to 63
- cell_time_bins: int32 [2, 2], replicated, may hold values from 0 to 999
- frozen: bfloat16 [4, 4096, 2048], P('pipe', 'dp'), may hold values from -0.09375 to 0.09375
- section_norm_gain: float32 [4, 4096], P('pipe'), may hold values from 0.5 to 1.5
- adapter_into_rank: bfloat16 [4, 4096, 64], P('pipe'), may hold values from -0.09375 to 0.09375
- adapter_onto_hidden: bfloat16 [4, 64, 2048], P('pipe'), may hold values from -0.75 to 0.75
- adapter_hidden_to_rank: bfloat16 [4, 2048, 64], P('pipe'), may hold values from -0.125 to 0.125
- adapter_to_width: bfloat16 [4, 64, 4096], P('pipe'), may hold values from -0.75 to 0.75
Outputs:
- grad_gain: float32 [4, 4096], P('pipe')
- grad_in: float32 [4, 4096, 64], P('pipe')
- grad_up: float32 [4, 64, 2048], P('pipe')
- grad_mix: float32 [4, 2048, 64], P('pipe')
- grad_out: float32 [4, 64, 4096], P('pipe')
The draws below stay inside these ranges and needn't reach their ends.
Inputs may be any that keep to these rules, and one draw needn't show every extreme that they name: `owners`: in each micro-batch, the 64 rows of one device of dp name no owner more than 4 times, a bound that some block reaches in some such rows.
All inputs are finite; a program needn't handle non-finite values.
Results may differ from the reference program's by a relative error of at most 0.0045.
Values may be sent and summed in bfloat16 or wider, within the bound.
No kernel may reach another device: no remote copies, remote signals or barrier semaphores. Data moves between devices by JAX's collectives and lax.ppermute only.
A program may use at most 128 MiB of HBM per device.

```python
import math
import jax
import jax.numpy as jnp
import numpy as np
from jax import lax

MODEL_WIDTH = 4096
HIDDEN_UNITS = 2048
ADAPTER_RANK = 64
MB = 2
TOK_MB = 64
CELLS = 2
NBINS = 1000
RELAY_SECTIONS = 4
TOKENS = 4096
CELL_LEN = 2048
CAP = 4
N_DP = 64


def plant(array, rng, least, high):
    shape = array.shape
    place = [jax.random.randint(jax.random.fold_in(rng, axis), (), 0, shape[axis]) for axis in range(len(shape))]
    array = array.at[tuple(place)].set(least)
    longest = shape.index(max(shape))
    place[longest] = (place[longest] + 1) % shape[longest]
    return array.at[tuple(place)].set(high)


def levels(rng, shape, pieces, least, largest):
    level = 1.0
    for dim, blocks in pieces:
        draws = jax.random.uniform(jax.random.fold_in(jax.random.fold_in(rng, 6), dim), (blocks,), jnp.float32, least / len(pieces), largest / len(pieces))
        level = level * jnp.repeat(jnp.exp(draws), shape[dim] // blocks).reshape((-1,) + (1,) * (len(shape) - 1 - dim))
    return level


def deal_out(own_key, own, number, rows, count, top, most, lean):
    ranking = jax.random.permutation(own_key, count)
    heavy_load, usual = portions_of(count, rows * top, most, lean, True), portions_of(count, rows * top, most, lean, False)
    places = jnp.arange(count)

    def named(sizes, turn):
        used = int((sizes > 0).sum())
        fixed = max(1, used // 4)
        shifted = fixed + (places - fixed + turn * (used - fixed)) % max(1, count - fixed)
        return jnp.zeros((count,), jnp.int32).at[ranking[jnp.where(places < fixed, places, shifted)]].set(jnp.asarray(sizes, jnp.int32))

    sizes = jnp.where(number % 4 == 0, named(heavy_load, number // 4), named(usual, number - number // 4 - 1))
    mixed = jax.random.permutation(jax.random.fold_in(own, 3), count)
    donor, sink = mixed[0:count // 2 * 2:2], mixed[1:count // 2 * 2:2]
    margin = jnp.minimum(sizes[donor] - 1, most - sizes[sink]) // 2
    margin = jnp.where((donor == ranking[0]) | (sink == ranking[0]) | (sizes[sink] == 0), 0, jnp.maximum(margin, 0))
    shifted = jax.random.randint(jax.random.fold_in(own, 4), (count // 2,), 0, 1 << 20) % (margin + 1)
    sizes = sizes.at[donor].add(-shifted).at[sink].add(shifted)
    items = jnp.searchsorted(jnp.cumsum(sizes), jnp.arange(rows * top), side="right").astype(jnp.int32)
    listing = items.reshape(top, rows).T
    listing = listing[jax.random.permutation(jax.random.fold_in(own, 1), rows)]
    turn = jax.random.randint(jax.random.fold_in(own, 2), (rows, 1), 0, top)
    return jnp.take_along_axis(listing, (jnp.arange(top)[None, :] + turn) % top, axis=1)


def portions_of(amount, total, limit, lean, full):
    weights = [(1 << 20) // math.isqrt(standing ** lean) + 1 for standing in range(1, amount + 1)]
    largest = limit if full else min(limit, max(-(-total // amount), total * weights[0] // sum(weights)))
    least = 1 if total - largest >= amount - 1 else 0
    counts, rest = [largest] + [least] * (amount - 1), total - largest - least * (amount - 1)
    while rest > 0:
        free = [i for i in range(1, amount) if counts[i] < largest] or [i for i in range(1, amount) if counts[i] < limit]
        whole, remaining = sum([weights[i] for i in free]), rest
        for i in free:
            more = min(limit - counts[i], max(1, remaining * weights[i] // whole), rest)
            counts[i] = counts[i] + more
            rest = rest - more
    return np.array(counts)


def bell_draw(stream_key, shape, width, limit, cuts=(), kind=jnp.bfloat16):
    values = width * jax.random.normal(stream_key, shape, jnp.float32)
    if cuts:
        values = values * levels(stream_key, shape, cuts, -0.22, 0.18)
    return jnp.clip(values, -limit, limit).astype(kind)


def setup_inputs(seed: int = 0) -> dict:
    arg_keys = jax.random.split(jax.random.key(seed), 12)
    perturbed = bell_draw(arg_keys[0], (MB, TOKENS, MODEL_WIDTH), 1.0, 6.0, ((1, 64),))
    control_token_states = bell_draw(arg_keys[1], (MB, TOKENS, MODEL_WIDTH), 1.0, 6.0, ((1, 64),))
    owners_keys = jax.random.split(jax.random.fold_in(arg_keys[2], 1), MB * TOKENS // TOK_MB)
    owners_turns = jax.random.permutation(jax.random.fold_in(arg_keys[2], 3), MB * TOKENS // TOK_MB)
    owners = jax.vmap(lambda own, number: deal_out(jax.random.fold_in(arg_keys[2], 2), own, number, TOK_MB, N_DP, 1, CAP, 2))(owners_keys, owners_turns).reshape((MB, TOKENS, 1))
    matched_control_row = plant(jax.random.randint(arg_keys[3], (MB, TOKENS), 0, TOK_MB), jax.random.fold_in(arg_keys[3], 1), 0, TOK_MB - 1).astype(jnp.int32)
    cell_time_bins = plant(jax.random.randint(arg_keys[4], (MB, CELLS), 0, NBINS), jax.random.fold_in(arg_keys[4], 1), 0, NBINS - 1).astype(jnp.int32)
    frozen = bell_draw(arg_keys[5], (RELAY_SECTIONS, MODEL_WIDTH, HIDDEN_UNITS), MODEL_WIDTH ** -0.5, 0.09375, ((0, 4), (1, 64)))
    section_norm_gain = jnp.clip(1.0 + 0.1 * jax.random.normal(arg_keys[6], (RELAY_SECTIONS, MODEL_WIDTH), jnp.float32), 0.5, 1.5)
    adapter_into_rank = bell_draw(arg_keys[7], (RELAY_SECTIONS, MODEL_WIDTH, ADAPTER_RANK), MODEL_WIDTH ** -0.5, 0.09375, ((0, 4),))
    adapter_onto_hidden = bell_draw(arg_keys[8], (RELAY_SECTIONS, ADAPTER_RANK, HIDDEN_UNITS), ADAPTER_RANK ** -0.5, 0.75, ((0, 4),))
    adapter_hidden_to_rank = bell_draw(arg_keys[9], (RELAY_SECTIONS, HIDDEN_UNITS, ADAPTER_RANK), HIDDEN_UNITS ** -0.5, 0.125, ((0, 4),))
    adapter_to_width = bell_draw(arg_keys[10], (RELAY_SECTIONS, ADAPTER_RANK, MODEL_WIDTH), ADAPTER_RANK ** -0.5, 0.75, ((0, 4),))
    return {"perturbed": perturbed, "control_token_states": control_token_states, "owners": owners, "matched_control_row": matched_control_row, "cell_time_bins": cell_time_bins, "frozen": frozen, "section_norm_gain": section_norm_gain, "adapter_into_rank": adapter_into_rank, "adapter_onto_hidden": adapter_onto_hidden, "adapter_hidden_to_rank": adapter_hidden_to_rank, "adapter_to_width": adapter_to_width}


epsilon = 1e-05

def times_transposed(left, right):
    return lax.dot_general(left, right, (((1,), (1,)), ((), ())), preferred_element_type=jnp.float32)

def transposed_times(left, right):
    return lax.dot_general(left, right, (((0,), (0,)), ((), ())), preferred_element_type=jnp.float32)

def time_features(t_val, width_dim):
    half_width = width_dim // 2
    frequency = jnp.exp(-jnp.log(10000.0) * jnp.arange(half_width, dtype=jnp.float32) / half_width)
    angles = (t_val * 1000.0)[:, None] * frequency[None, :]
    return jnp.concatenate([jnp.sin(angles), jnp.cos(angles)], axis=1)

def section_forward_pass(residual_state, gain_vector_row, frozen_weight_rows, adapter_down_first, adapter_up_first, adapter_down_second, adapter_up_second):
    hidden_widened = residual_state.astype(jnp.float32)
    inverse = lax.rsqrt(lax.optimization_barrier(jnp.mean(hidden_widened * hidden_widened, axis=1, keepdims=True)) + epsilon)
    normalized_state = (hidden_widened * inverse * gain_vector_row[None, :]).astype(jnp.bfloat16)
    rank_projected = jnp.dot(normalized_state, adapter_down_first, preferred_element_type=jnp.float32).astype(jnp.bfloat16)
    mixed_preactivation = jnp.dot(normalized_state, frozen_weight_rows, preferred_element_type=jnp.float32) + jnp.dot(rank_projected, adapter_up_first, preferred_element_type=jnp.float32)
    hidden_units_value = jax.nn.silu(mixed_preactivation).astype(jnp.bfloat16)
    rank_squeezed = jnp.dot(hidden_units_value, adapter_down_second, preferred_element_type=jnp.float32).astype(jnp.bfloat16)
    section_result = (hidden_widened + jnp.dot(rank_squeezed, adapter_up_second, preferred_element_type=jnp.float32)).astype(jnp.bfloat16)
    return (section_result, (inverse, normalized_state, rank_projected, mixed_preactivation, hidden_units_value, rank_squeezed))

def section_backward_pass(residual_state, saved_activations, upstream_gradient, gain_vector_row, frozen_weight_rows, adapter_down_first, adapter_up_first, adapter_down_second, adapter_up_second):
    inverse, normalized_state, rank_projected, mixed_preactivation, hidden_units_value, rank_squeezed = saved_activations
    grad_e = transposed_times(rank_squeezed, upstream_gradient)
    squeezed_gradient = times_transposed(upstream_gradient, adapter_up_second).astype(jnp.bfloat16)
    grad_c = transposed_times(hidden_units_value, squeezed_gradient)
    hidden_gradient = times_transposed(squeezed_gradient, adapter_down_second)
    sigmoid_val = jax.nn.sigmoid(mixed_preactivation)
    preact_gradient = (hidden_gradient * sigmoid_val * (1.0 + mixed_preactivation * (1.0 - sigmoid_val))).astype(jnp.bfloat16)
    grad_b = transposed_times(rank_projected, preact_gradient)
    lowered_gradient = times_transposed(preact_gradient, adapter_up_first).astype(jnp.bfloat16)
    grad_a = transposed_times(normalized_state, lowered_gradient)
    normed_gradient = times_transposed(preact_gradient, frozen_weight_rows) + times_transposed(lowered_gradient, adapter_down_first)
    unit_rows = residual_state.astype(jnp.float32) * inverse
    grad_g = lax.optimization_barrier(jnp.sum(normed_gradient * unit_rows, axis=0))
    d_unit = normed_gradient * gain_vector_row[None, :]
    d_stream = inverse * (d_unit - unit_rows * lax.optimization_barrier(jnp.mean(d_unit * unit_rows, axis=1, keepdims=True)))
    upstream = (upstream_gradient.astype(jnp.float32) + d_stream).astype(jnp.bfloat16)
    return (upstream, (grad_g, grad_a, grad_b, grad_c, grad_e))

def reference(perturbed, control_token_states, owners, matched_control_row, cell_time_bins, frozen, section_norm_gain, adapter_into_rank, adapter_onto_hidden, adapter_hidden_to_rank, adapter_to_width):
    loss_scale = (MB * TOKENS) ** (-0.5)
    position = jnp.arange(TOKENS, dtype=jnp.int32)
    gradient_totals = [[jnp.zeros(section_norm_gain.shape[1:], jnp.float32), jnp.zeros(adapter_into_rank.shape[1:], jnp.float32), jnp.zeros(adapter_onto_hidden.shape[1:], jnp.float32), jnp.zeros(adapter_hidden_to_rank.shape[1:], jnp.float32), jnp.zeros(adapter_to_width.shape[1:], jnp.float32)] for relay_section_index in range(RELAY_SECTIONS)]
    for batch_index in range(MB):
        row_ids = (owners[batch_index, :, 0] * TOK_MB + matched_control_row[batch_index]).astype(jnp.int32)
        source_rows = jnp.take(control_token_states[batch_index], row_ids, axis=0).astype(jnp.float32)
        target_rows = perturbed[batch_index].astype(jnp.float32)
        bin_vals = jnp.take(cell_time_bins[batch_index], (position // CELL_LEN).astype(jnp.int32), axis=0)
        t_val = (bin_vals.astype(jnp.float32) + 0.5) / NBINS
        residual_state = ((1.0 - t_val)[:, None] * source_rows + t_val[:, None] * target_rows + time_features(t_val, MODEL_WIDTH)).astype(jnp.bfloat16)
        velocity = target_rows - source_rows
        history = []
        for relay_section_index in range(RELAY_SECTIONS):
            relay_section_weights = (section_norm_gain[relay_section_index], frozen[relay_section_index], adapter_into_rank[relay_section_index], adapter_onto_hidden[relay_section_index], adapter_hidden_to_rank[relay_section_index], adapter_to_width[relay_section_index])
            section_result, saved_activations = section_forward_pass(residual_state, *relay_section_weights)
            history.append((residual_state, saved_activations))
            residual_state = section_result
        upstream_gradient = ((residual_state.astype(jnp.float32) - velocity) * loss_scale).astype(jnp.bfloat16)
        for relay_section_index in reversed(range(RELAY_SECTIONS)):
            relay_section_weights = (section_norm_gain[relay_section_index], frozen[relay_section_index], adapter_into_rank[relay_section_index], adapter_onto_hidden[relay_section_index], adapter_hidden_to_rank[relay_section_index], adapter_to_width[relay_section_index])
            upstream_gradient, grad_terms = section_backward_pass(history[relay_section_index][0], history[relay_section_index][1], upstream_gradient, *relay_section_weights)
            gradient_totals[relay_section_index] = [gradient_totals[relay_section_index][k] + grad_terms[k] for k in range(5)]
    return tuple((jnp.stack([gradient_totals[relay_section_index][k] for relay_section_index in range(RELAY_SECTIONS)]) for k in range(5)))
```

```python
import jax
import jax.numpy as jnp
from jax import lax
from jax.experimental import pallas as pl
from jax.experimental.pallas import tpu as pltpu
from jax.sharding import Mesh
from jax.sharding import PartitionSpec as P

NBINS = 1000
EPSILON = 1e-05
TOKENS = 128
WIDTH = 4096
HIDDEN = 2048
RANK = 64
SECTIONS = 4
WIDE = 512
NARROW = 256
DP = ("z", "x", "core")
F32 = jnp.float32
BF16 = jnp.bfloat16
VMEM = pl.BlockSpec(memory_space=pltpu.VMEM)
SMEM = pl.BlockSpec(memory_space=pltpu.SMEM)
PARAMS = pltpu.CompilerParams(vmem_limit_bytes=24 << 20)


def nn(left, right):
    return jnp.dot(left, right, preferred_element_type=F32)


def nt(left, right):
    return lax.dot_general(left, right, (((1,), (1,)), ((), ())), preferred_element_type=F32)


def tn(left, right):
    return lax.dot_general(left, right, (((0,), (0,)), ((), ())), preferred_element_type=F32)


def call(kernel, outs, args, scratch=(), smem=0):
    specs = [SMEM] * smem + [VMEM] * (len(args) - smem)
    out_shape = tuple(jax.ShapeDtypeStruct(s, d) for s, d in outs)
    return pl.pallas_call(
        kernel,
        in_specs=specs,
        out_specs=tuple(VMEM for _ in outs),
        out_shape=out_shape,
        scratch_shapes=[pltpu.VMEM(s, d) for s, d in scratch],
        compiler_params=PARAMS,
    )(*args)


def blocks(total, size):
    return [slice(i, i + size) for i in range(0, total, size)]


def entry_kernel(time_ref, source_ref, target_ref, feature_ref, out_ref):
    for batch in range(2):
        rows = slice(batch * 64, batch * 64 + 64)
        t = time_ref[batch]
        for q in range(SECTIONS):
            cols = slice(q * 1024, q * 1024 + 1024)
            source = source_ref[q, rows, :].astype(F32)
            target = target_ref[rows, cols].astype(F32)
            feature = feature_ref[batch : batch + 1, cols]
            out_ref[rows, cols] = ((1.0 - t) * source + t * target + feature).astype(BF16)


def forward_body(plane, x0, squeezed_in, widths, gain, frozen, into, onto, back, xs, normed):
    total = jnp.zeros((TOKENS, 1), F32)
    for cols in blocks(WIDTH, WIDE):
        x = x0[:, cols].astype(F32)
        for j in range(SECTIONS - 1):
            x = (x + nn(squeezed_in[j], widths[j, :, cols])).astype(BF16).astype(F32)
        xs[:, cols] = x.astype(BF16)
        total = total + jnp.sum(x * x, axis=1, keepdims=True)
    inverse = lax.rsqrt(total * (1.0 / WIDTH) + EPSILON)
    lowered = jnp.zeros((TOKENS, RANK), F32)
    for cols in blocks(WIDTH, WIDE):
        value = (xs[:, cols].astype(F32) * inverse * gain[:, cols]).astype(BF16)
        normed[:, cols] = value
        lowered = lowered + nt(value, into[:, cols])
    lowered = lowered.astype(BF16)
    return inverse, lowered


def forward_kernel(plane, x0, squeezed_in, widths, gain, frozen, into, onto, back, out, xs, normed):
    _, lowered = forward_body(plane, x0, squeezed_in, widths, gain, frozen, into, onto, back, xs, normed)
    squeezed = jnp.zeros((TOKENS, RANK), F32)
    for cols in blocks(HIDDEN, NARROW):
        pre = nn(normed[...], frozen[:, cols]) + nn(lowered, onto[:, cols])
        hidden = (pre * jax.nn.sigmoid(pre)).astype(BF16)
        squeezed = squeezed + nt(hidden, back[:, cols])
    squeezed = squeezed.astype(BF16)
    for j in range(SECTIONS - 1):
        out[j] = jnp.where(plane[0] == j, squeezed, squeezed_in[j])


def forward_last_kernel(
    plane, x0, squeezed_in, widths, gain, frozen, into, onto, back, own_width, source, target,
    xs, normed, inverse_out, lowered_out, slope, hidden_out, squeezed_out, seed, projected,
):
    inverse, lowered = forward_body(plane, x0, squeezed_in, widths, gain, frozen, into, onto, back, xs, normed)
    inverse_out[...] = inverse
    lowered_out[...] = lowered
    squeezed = jnp.zeros((TOKENS, RANK), F32)
    for cols in blocks(HIDDEN, NARROW):
        pre = nn(normed[...], frozen[:, cols]) + nn(lowered, onto[:, cols])
        sigmoid = jax.nn.sigmoid(pre)
        hidden = (pre * sigmoid).astype(BF16)
        slope[:, cols] = sigmoid * (1.0 + pre * (1.0 - sigmoid))
        hidden_out[:, cols] = hidden
        squeezed = squeezed + nt(hidden, back[:, cols])
    squeezed = squeezed.astype(BF16)
    squeezed_out[...] = squeezed
    scale = 8192.0 ** (-0.5)
    sums = [jnp.zeros((TOKENS, RANK), F32) for _ in range(SECTIONS)]
    for i, cols in enumerate(blocks(WIDTH, WIDE)):
        prediction = (xs[:, cols].astype(F32) + nn(squeezed, own_width[:, cols])).astype(BF16).astype(F32)
        part = slice((i % 2) * WIDE, (i % 2) * WIDE + WIDE)
        velocity = target[:, cols].astype(F32) - source[i // 2, :, part].astype(F32)
        value = ((prediction - velocity) * scale).astype(BF16)
        seed[:, cols] = value
        for j in range(SECTIONS):
            sums[j] = sums[j] + nt(value, widths[j, :, cols])
    for j in range(SECTIONS):
        projected[j] = sums[j]


def backward_body(plane, received, projected, back, slope, onto, frozen, into, xs, inverse, gain, d_pre, d_unit, gain_out):
    last = plane[0] == SECTIONS - 1
    own = received[jnp.minimum(plane[0], SECTIONS - 2)]
    d_squeezed = jnp.where(last, projected[SECTIONS - 1], own).astype(BF16)
    d_lowered = jnp.zeros((TOKENS, RANK), F32)
    for cols in blocks(HIDDEN, NARROW):
        value = (nn(d_squeezed, back[:, cols]) * slope[:, cols]).astype(BF16)
        d_pre[:, cols] = value
        d_lowered = d_lowered + nt(value, onto[:, cols])
    d_lowered = d_lowered.astype(BF16)
    total = jnp.zeros((TOKENS, 1), F32)
    for cols in blocks(WIDTH, WIDE):
        d_normed = nt(d_pre[...], frozen[cols, :]) + nn(d_lowered, into[:, cols])
        unit = xs[:, cols].astype(F32) * inverse[...]
        if gain_out is not None:
            gain_out[:, cols] = jnp.sum(d_normed * unit, axis=0, keepdims=True)
        else:
            value = d_normed * gain[:, cols]
            d_unit[:, cols] = value
            total = total + jnp.sum(value * unit, axis=1, keepdims=True)
    return d_squeezed, d_lowered, total


def backward_kernel(
    plane, received, projected, back, slope, onto, frozen, into, xs, inverse, gain, widths,
    out, d_stream, d_pre,
):
    _, _, total = backward_body(
        plane, received, projected, back, slope, onto, frozen, into, xs, inverse, gain, d_pre, d_stream, None
    )
    mean = total * (1.0 / WIDTH)
    sums = [jnp.zeros((TOKENS, RANK), F32) for _ in range(SECTIONS - 1)]
    for cols in blocks(WIDTH, WIDE):
        unit = xs[:, cols].astype(F32) * inverse[...]
        value = inverse[...] * (d_stream[:, cols] - unit * mean)
        d_stream[:, cols] = value
        narrow = value.astype(BF16)
        for j in range(SECTIONS - 1):
            sums[j] = sums[j] + nt(narrow, widths[j, :, cols])
    last = plane[0] == SECTIONS - 1
    for j in range(SECTIONS - 1):
        out[j] = jnp.where(last, projected[j], received[j]) + sums[j]


def backward_last_kernel(
    plane, received, projected, back, slope, onto, frozen, into, xs, inverse, gain, normed, lowered, hidden,
    keep, send, d_pre, gain_row, grads,
):
    d_squeezed, d_lowered, _ = backward_body(
        plane, received, projected, back, slope, onto, frozen, into, xs, inverse, gain, d_pre, None, gain_row
    )
    for cols in blocks(WIDTH, WIDE):
        grads[:, cols] = tn(d_lowered, normed[:, cols])
    for cols in blocks(HIDDEN, WIDE):
        grads[:, 4096 + cols.start : 4096 + cols.stop] = tn(lowered[...], d_pre[:, cols])
        grads[:, 6144 + cols.start : 6144 + cols.stop] = tn(d_squeezed, hidden[:, cols])
    grads[:, 8192:9216] = jnp.zeros((RANK, 1024), F32)
    for q in range(4):
        grads[q : q + 1, 8192:9216] = gain_row[:, q * 1024 : q * 1024 + 1024]
    half = grads.shape[1] // 2
    core = plane[1]
    keep[...] = grads[:, pl.ds(pl.multiple_of(core * half, 128), half)]
    send[...] = grads[:, pl.ds(pl.multiple_of((1 - core) * half, 128), half)]


def outward_kernel(plane, squeezed, cotangent, keep, send, grads):
    for cols in blocks(WIDTH, WIDE):
        grads[:, cols] = tn(squeezed[...], cotangent[:, cols])
    half = grads.shape[1] // 2
    core = plane[1]
    keep[...] = grads[:, pl.ds(pl.multiple_of(core * half, 128), half)]
    send[...] = grads[:, pl.ds(pl.multiple_of((1 - core) * half, 128), half)]


def exchange(x, axis):
    return lax.all_to_all(x, axis, split_axis=0, concat_axis=0, tiled=True)


def copies(x, count):
    return jnp.broadcast_to(x[None], (count,) + x.shape)


SWAP = [(0, 1), (1, 0)]


def summed_over_dp(keep, send):
    columns = keep.shape[1] // 4
    mine = keep + lax.ppermute(send, "core", SWAP)
    parts = mine.reshape(RANK, 4, columns).transpose(1, 0, 2)
    along_x = jnp.sum(exchange(parts, "x"), axis=0)
    along_z = jnp.sum(exchange(along_x.reshape(8, 8, columns), "z"), axis=0)
    rows = exchange(copies(along_z, 8), "z").reshape(RANK, columns)
    half = exchange(copies(rows, 4), "x").transpose(1, 0, 2).reshape(RANK, 4 * columns)
    other = lax.ppermute(half, "core", SWAP)
    first = lax.axis_index("core") == 0
    return jnp.concatenate([jnp.where(first, half, other), jnp.where(first, other, half)], axis=1)


def per_device(
    perturbed,
    control_token_states,
    owners,
    matched_control_row,
    cell_time_bins,
    frozen,
    section_norm_gain,
    adapter_into_rank,
    adapter_onto_hidden,
    adapter_hidden_to_rank,
    adapter_to_width,
):
    plane = lax.axis_index("pipe")
    position = lax.axis_index(DP)
    places = jnp.stack([plane, lax.axis_index("core")]).astype(jnp.int32)

    weights = lax.all_gather(frozen[0], DP, axis=0, tiled=True)

    names = owners[:, :, 0]
    same = (names[:, :, None] == names[:, None, :]) & jnp.tril(jnp.ones((64, 64), bool), -1)[None]
    rank = jnp.sum(same.astype(jnp.int32), axis=2)
    batch = jnp.arange(2, dtype=jnp.int32)[:, None]
    slot = (names * 8 + batch * 4 + rank).reshape(TOKENS)
    row = (batch * 64 + matched_control_row).reshape(TOKENS)
    chosen = slot[:, None] == jnp.arange(512, dtype=jnp.int32)[None, :]
    table = jnp.sum(jnp.where(chosen, row[:, None], 0), axis=0).reshape(64, 8)
    asked = exchange(table, DP).reshape(512)

    pool = control_token_states.reshape(TOKENS, WIDTH)
    quarter = lax.dynamic_slice_in_dim(pool, plane * 1024, 1024, axis=1)
    picked = nn((asked[:, None] == jnp.arange(TOKENS, dtype=jnp.int32)[None, :]).astype(BF16), quarter)
    arrived = exchange(picked.astype(BF16).reshape(64, 8, 1024), DP).reshape(512, 1024)
    own_quarter = nn(chosen.astype(BF16), arrived).astype(BF16)
    source = exchange(copies(own_quarter, SECTIONS), "pipe")
    widths = exchange(copies(adapter_to_width[0], SECTIONS), "pipe")

    cell = position // 32
    bins = jnp.where(cell == 0, cell_time_bins[:, 0], cell_time_bins[:, 1])
    t_val = (bins.astype(F32) + 0.5) / NBINS
    frequency = jnp.exp(-jnp.log(10000.0) * jnp.arange(WIDTH // 2, dtype=F32) / (WIDTH // 2))
    angles = (t_val * 1000.0)[:, None] * frequency[None, :]
    features = jnp.concatenate([jnp.sin(angles), jnp.cos(angles)], axis=1)
    target = perturbed.reshape(TOKENS, WIDTH)
    (x0,) = call(entry_kernel, [((TOKENS, WIDTH), BF16)], [t_val, source, target, features], smem=1)

    gain = section_norm_gain
    into = adapter_into_rank[0].T
    onto = adapter_onto_hidden[0]
    back = adapter_hidden_to_rank[0].T
    own_width = adapter_to_width[0]
    stream = ((TOKENS, WIDTH), BF16)
    down = [(i, i + 1) for i in range(SECTIONS - 1)]
    up = [(i + 1, i) for i in range(SECTIONS - 1)]

    squeezed_in = jnp.zeros((SECTIONS - 1, TOKENS, RANK), BF16)
    for _ in range(SECTIONS - 1):
        (squeezed_out,) = call(
            forward_kernel,
            [((SECTIONS - 1, TOKENS, RANK), BF16)],
            [places, x0, squeezed_in, widths, gain, weights, into, onto, back],
            scratch=[stream, stream],
            smem=1,
        )
        squeezed_in = lax.ppermute(squeezed_out, "pipe", down)
    xs, normed, inverse, lowered, slope, hidden, squeezed, seed, projected = call(
        forward_last_kernel,
        [
            stream,
            stream,
            ((TOKENS, 1), F32),
            ((TOKENS, RANK), BF16),
            ((TOKENS, HIDDEN), F32),
            ((TOKENS, HIDDEN), BF16),
            ((TOKENS, RANK), BF16),
            stream,
            ((SECTIONS, TOKENS, RANK), F32),
        ],
        [places, x0, squeezed_in, widths, gain, weights, into, onto, back, own_width, source, target],
        smem=1,
    )

    is_last = plane == SECTIONS - 1
    received = jnp.zeros((SECTIONS - 1, TOKENS, RANK), F32)
    cotangent = seed
    for _ in range(SECTIONS - 1):
        sent, d_stream = call(
            backward_kernel,
            [((SECTIONS - 1, TOKENS, RANK), F32), ((TOKENS, WIDTH), F32)],
            [places, received, projected, back, slope, onto, weights, into, xs, inverse, gain, widths],
            scratch=[((TOKENS, HIDDEN), BF16)],
            smem=1,
        )
        received = lax.ppermute(sent, "pipe", up)
        handed = (cotangent.astype(F32) + d_stream).astype(BF16)
        cotangent = jnp.where(is_last, seed, lax.ppermute(handed, "pipe", up))
    keep, send = call(
        backward_last_kernel,
        [((RANK, 4608), F32)] * 2,
        [places, received, projected, back, slope, onto, weights, into, xs, inverse, gain, normed, lowered, hidden],
        scratch=[((TOKENS, HIDDEN), BF16), ((1, WIDTH), F32), ((RANK, 9216), F32)],
        smem=1,
    )
    inner = summed_over_dp(keep, send)
    keep, send = call(
        outward_kernel,
        [((RANK, 2048), F32)] * 2,
        [places, squeezed, cotangent],
        scratch=[((RANK, WIDTH), F32)],
        smem=1,
    )
    outer = summed_over_dp(keep, send)
    return (
        inner[:4, 8192:].reshape(1, WIDTH),
        inner[:, :4096].T[None],
        inner[:, 4096:6144][None],
        inner[:, 6144:8192].T[None],
        outer[None],
    )


def solution(mesh):
    cells = Mesh(mesh.devices.reshape(8, 4, 2, 4), ("z", "x", "core", "pipe"))
    in_specs = (
        P(None, DP, None),
        P(None, DP, None),
        P(None, DP, None),
        P(None, DP),
        P(),
        P("pipe", DP, None),
        P("pipe", None),
        P("pipe", None, None),
        P("pipe", None, None),
        P("pipe", None, None),
        P("pipe", None, None),
    )
    out_specs = (
        P("pipe", None),
        P("pipe", None, None),
        P("pipe", None, None),
        P("pipe", None, None),
        P("pipe", None, None),
    )
    return jax.shard_map(per_device, mesh=cells, in_specs=in_specs, out_specs=out_specs, check_vma=False)
```

```python
import functools

import jax
import jax.numpy as jnp
from jax import lax
from jax.experimental import pallas as pl
from jax.experimental.pallas import tpu as pltpu
from jax.sharding import Mesh
from jax.sharding import PartitionSpec as P

NBINS = 1000
EPSILON = 1e-05
TOKENS = 128
WIDTH = 4096
HIDDEN = 2048
RANK = 64
SECTIONS = 4
WIDE = 512
NARROW = 256
DP = ("z", "x", "core")
F32 = jnp.float32
BF16 = jnp.bfloat16
VMEM = pl.BlockSpec(memory_space=pltpu.VMEM)
SMEM = pl.BlockSpec(memory_space=pltpu.SMEM)
HBM = pl.BlockSpec(memory_space=pltpu.HBM)
PARTS = (1536, 1536, 1024)


def nn(left, right):
    return jnp.dot(left, right, preferred_element_type=F32)


def nt(left, right):
    return lax.dot_general(left, right, (((1,), (1,)), ((), ())), preferred_element_type=F32)


def tn(left, right):
    return lax.dot_general(left, right, (((0,), (0,)), ((), ())), preferred_element_type=F32)


def packed(value):
    return jnp.concatenate([value[0:64], value[64:128]], axis=1)


def unpacked(value):
    return jnp.concatenate([value[:, 0:64], value[:, 64:128]], axis=0)


def call(kernel, outs, args, scratch=(), smem=0, hbm=(), limit=8, cost=1):
    specs = [SMEM if i < smem else HBM if i in hbm else VMEM for i in range(len(args))]
    out_shape = tuple(jax.ShapeDtypeStruct(s, d) for s, d in outs)
    return pl.pallas_call(
        kernel,
        in_specs=specs,
        out_specs=tuple(VMEM for _ in outs),
        out_shape=out_shape,
        scratch_shapes=[s if hasattr(s, "memory_space") else pltpu.VMEM(*s) for s in scratch],
        cost_estimate=pl.CostEstimate(
            flops=cost * 10**9, bytes_accessed=cost * 3 * 10**6, transcendentals=0
        ),
        compiler_params=pltpu.CompilerParams(vmem_limit_bytes=limit << 20),
    )(*args)


def blocks(total, size):
    return [slice(i, i + size) for i in range(0, total, size)]


def entry_kernel(time_ref, source_ref, target_ref, feature_ref, out_ref):
    for batch in range(2):
        rows = slice(batch * 64, batch * 64 + 64)
        t = time_ref[batch]
        for q in range(SECTIONS):
            cols = slice(q * 1024, q * 1024 + 1024)
            source = source_ref[q, rows, :].astype(F32)
            target = target_ref[rows, cols].astype(F32)
            feature = feature_ref[batch : batch + 1, cols]
            out_ref[rows, cols] = ((1.0 - t) * source + t * target + feature).astype(BF16)


def widths_kernel(plane, own, one, two, three, out):
    for j in range(SECTIONS):
        for cols in blocks(WIDTH, WIDE):
            value = jnp.where(plane[0] == j, own[:, cols].astype(F32), 0.0)
            for k, part in ((1, one), (2, two), (3, three)):
                value = jnp.where(plane[0] == j + k, part[:, cols].astype(F32), value)
            out[j, :, cols] = value.astype(BF16)


def forward_body(x0, squeezed_in, widths, gain, into, xs, normed):
    total = jnp.zeros((TOKENS, 1), F32)
    steps = [unpacked(step.astype(F32)).astype(BF16) for step in squeezed_in]
    for cols in blocks(WIDTH, WIDE):
        x = x0[:, cols].astype(F32)
        for j, step in enumerate(steps):
            x = (x + nn(step, widths[j, :, cols])).astype(BF16).astype(F32)
        if xs is not x0:
            xs[:, cols] = x.astype(BF16)
        total = total + jnp.sum(x * x, axis=1, keepdims=True)
    inverse = lax.rsqrt(total * (1.0 / WIDTH) + EPSILON)
    lowered = jnp.zeros((TOKENS, RANK), F32)
    for cols in blocks(WIDTH, WIDE):
        value = (xs[:, cols].astype(F32) * inverse * gain[:, cols]).astype(BF16)
        normed[:, cols] = value
        lowered = lowered + nt(value, into[:, cols])
    lowered = lowered.astype(BF16)
    return inverse, lowered


def forward_tail(plane, tick, squeezed_in, lowered, normed, frozen, onto, back, out, arrived):
    squeezed = jnp.zeros((TOKENS, RANK), F32)
    for i, cols in enumerate(blocks(HIDDEN, NARROW)):
        arrived(i)
        pre = nn(normed[...], frozen[:, cols]) + nn(lowered, onto[:, cols])
        hidden = (pre * jax.nn.sigmoid(pre)).astype(BF16)
        squeezed = squeezed + nt(hidden, back[:, cols])
    squeezed = packed(squeezed)
    for j in range(tick):
        out[j] = jnp.where(plane[0] == j, squeezed, squeezed_in[j].astype(F32)).astype(BF16)
    out[tick] = jnp.where(plane[0] == tick, squeezed, 0.0).astype(BF16)


def forward_first_kernel(plane, x0, gain, weights, into, onto, back, out, frozen, normed, sems):
    moves = [
        pltpu.make_async_copy(weights.at[:, cols], frozen.at[:, cols], sems.at[i])
        for i, cols in enumerate(blocks(HIDDEN, NARROW))
    ]
    for move in moves:
        move.start()
    _, lowered = forward_body(x0, [], None, gain, into, x0, normed)
    forward_tail(plane, 0, None, lowered, normed, frozen, onto, back, out, lambda i: moves[i].wait())


def forward_kernel(tick, plane, x0, squeezed_in, widths, gain, frozen, into, onto, back, out, xs, normed):
    _, lowered = forward_body(x0, [squeezed_in[j] for j in range(tick)], widths, gain, into, xs, normed)
    forward_tail(plane, tick, squeezed_in, lowered, normed, frozen, onto, back, out, lambda i: None)


def transpose_kernel(first, rows, frozen, after, out):
    for r in range(0, rows, 256):
        for cols in blocks(HIDDEN, WIDE):
            out[cols, r : r + 256] = frozen[first + r : first + r + 256, cols].T


def forward_last_kernel(
    plane, x0, squeezed_in, widths, gain, frozen, into, onto, back, own_width, source, target,
    xs, normed, inverse_out, lowered_out, slope, hidden_out, squeezed_out, seed, projected,
):
    steps = [squeezed_in[j] for j in range(SECTIONS - 1)]
    inverse, lowered = forward_body(x0, steps, widths, gain, into, xs, normed)
    inverse_out[...] = inverse
    lowered_out[...] = lowered
    squeezed = jnp.zeros((TOKENS, RANK), F32)
    for cols in blocks(HIDDEN, NARROW):
        pre = nn(normed[...], frozen[:, cols]) + nn(lowered, onto[:, cols])
        sigmoid = jax.nn.sigmoid(pre)
        hidden = (pre * sigmoid).astype(BF16)
        slope[:, cols] = sigmoid * (1.0 + pre * (1.0 - sigmoid))
        hidden_out[:, cols] = hidden
        squeezed = squeezed + nt(hidden, back[:, cols])
    squeezed = squeezed.astype(BF16)
    squeezed_out[...] = squeezed
    scale = 8192.0 ** (-0.5)
    sums = [jnp.zeros((TOKENS, RANK), F32) for _ in range(SECTIONS)]
    for i, cols in enumerate(blocks(WIDTH, WIDE)):
        prediction = (xs[:, cols].astype(F32) + nn(squeezed, own_width[:, cols])).astype(BF16).astype(F32)
        part = slice((i % 2) * WIDE, (i % 2) * WIDE + WIDE)
        velocity = target[:, cols].astype(F32) - source[i // 2, :, part].astype(F32)
        value = ((prediction - velocity) * scale).astype(BF16)
        seed[:, cols] = value
        for j in range(SECTIONS):
            sums[j] = sums[j] + nt(value, widths[j, :, cols])
    for j in range(SECTIONS):
        projected[j] = sums[j]


def backward_body(d_squeezed, back, slope, onto, turned, into, xs, inverse, gain, d_pre, d_unit, gain_out):
    d_lowered = jnp.zeros((TOKENS, RANK), F32)
    for cols in blocks(HIDDEN, NARROW):
        value = (nn(d_squeezed, back[:, cols]) * slope[:, cols]).astype(BF16)
        d_pre[:, cols] = value
        d_lowered = d_lowered + nt(value, onto[:, cols])
    d_lowered = d_lowered.astype(BF16)
    total = jnp.zeros((TOKENS, 1), F32)
    for i, cols in enumerate(blocks(WIDTH, WIDE)):
        at = (i % 3) * WIDE
        d_normed = nn(d_pre[...], turned[i // 3][:, at : at + WIDE]) + nn(d_lowered, into[:, cols])
        unit = xs[:, cols].astype(F32) * inverse[...]
        if gain_out is not None:
            gain_out[:, cols] = jnp.sum(d_normed * unit, axis=0, keepdims=True)
        else:
            value = d_normed * gain[:, cols]
            d_unit[:, cols] = value
            total = total + jnp.sum(value * unit, axis=1, keepdims=True)
    return d_lowered, total


def backward_kernel(
    tick, plane, own, received, back, slope, onto, turned_a, turned_b, turned_c, into, xs, inverse, gain, widths,
    out, own_out, d_stream, d_pre,
):
    count = SECTIONS - 1 - tick
    base = [received[j] if tick == 0 else unpacked(received[j]) for j in range(count + (tick > 0))]
    if tick:
        own_out[...] = jnp.where(plane[0] == count, base[count], own[...])
    else:
        own_out[...] = own[SECTIONS - 1]
    turned = (turned_a, turned_b, turned_c)
    _, total = backward_body(
        own_out[...].astype(BF16), back, slope, onto, turned, into, xs, inverse, gain, d_pre, d_stream, None
    )
    mean = total * (1.0 / WIDTH)
    sums = [base[j] for j in range(count)]
    for cols in blocks(WIDTH, WIDE):
        unit = xs[:, cols].astype(F32) * inverse[...]
        value = inverse[...] * (d_stream[:, cols] - unit * mean)
        d_stream[:, cols] = value
        narrow = value.astype(BF16)
        for j in range(count):
            sums[j] = sums[j] + nt(narrow, widths[j, :, cols])
    for j in range(count):
        out[j] = packed(sums[j])


def hand_down_kernel(tick, plane, seed, d_stream, *rest):
    out = rest[-1]
    rows = pl.ds(pl.multiple_of(jnp.clip(tick - (SECTIONS - 1 - plane[0]), 0, 1) * 64, 64), 64)
    for cols in blocks(WIDTH, WIDE):
        held = seed[rows, cols].astype(F32)
        if len(rest) == 2:
            held = jnp.where(plane[0] == SECTIONS - 1, held, rest[0][:, cols].astype(F32))
        out[:, cols] = (held + d_stream[rows, cols]).astype(BF16)


def cut(grads, core, keep, send):
    piece = grads.shape[1] // 8
    for q in range(4):
        keep[q] = grads[:, pl.ds(pl.multiple_of((core * 4 + q) * piece, 128), piece)]
        send[q] = grads[:, pl.ds(pl.multiple_of(((1 - core) * 4 + q) * piece, 128), piece)]


def backward_last_kernel(
    plane, own, received, back, slope, onto, turned_a, turned_b, turned_c, into, xs, inverse, gain, normed, lowered,
    hidden, keep, send, d_pre, gain_row, grads,
):
    d_squeezed = jnp.where(plane[0] == 0, unpacked(received[0]), own[...]).astype(BF16)
    turned = (turned_a, turned_b, turned_c)
    d_lowered, _ = backward_body(
        d_squeezed, back, slope, onto, turned, into, xs, inverse, gain, d_pre, None, gain_row
    )
    for cols in blocks(WIDTH, WIDE):
        grads[:, cols] = tn(d_lowered, normed[:, cols])
    for cols in blocks(HIDDEN, WIDE):
        grads[:, 4096 + cols.start : 4096 + cols.stop] = tn(lowered[...], d_pre[:, cols])
        grads[:, 6144 + cols.start : 6144 + cols.stop] = tn(d_squeezed, hidden[:, cols])
    grads[:, 8192:9216] = jnp.zeros((RANK, 1024), F32)
    for q in range(4):
        grads[q : q + 1, 8192:9216] = gain_row[:, q * 1024 : q * 1024 + 1024]
    cut(grads, plane[1], keep, send)


def outward_kernel(plane, squeezed, seed, first, second, third, fourth, keep, send, grads):
    index = plane[0]
    for cols in blocks(WIDTH, WIDE):
        early = jnp.where(index == 2, first[:, cols], jnp.where(index == 1, second[:, cols], third[:, cols]))
        early = jnp.where(index == 3, seed[0:64, cols], early)
        late = jnp.where(index == 3, seed[64:128, cols], fourth[:, cols])
        grads[:, cols] = tn(squeezed[0:64, :], early) + tn(squeezed[64:128, :], late)
    cut(grads, plane[1], keep, send)


def add_kernel(left, right, out):
    for q in range(4):
        out[q] = left[q] + right[q]


def x_sum_kernel(inner, outer, out):
    out[:, 0:1152] = (inner[0] + inner[1]) + (inner[2] + inner[3])
    out[:, 1152:1664] = (outer[0] + outer[1]) + (outer[2] + outer[3])


def z_sum_kernel(parts, out):
    total = parts[0]
    for k in range(1, 8):
        total = total + parts[k]
    for k in range(8):
        out[k] = total


def repeat_kernel(rows, out):
    for q in range(4):
        out[q] = rows[...]


def outputs_kernel(plane, half, other, gain, into, onto, back, width, inner, outer):
    core = plane[1]
    for side, piece in ((core, half), (1 - core, other)):
        for q in range(4):
            inner[:, pl.ds(pl.multiple_of((side * 4 + q) * 1152, 128), 1152)] = piece[q, :, 0:1152]
            outer[:, pl.ds(pl.multiple_of((side * 4 + q) * 512, 128), 512)] = piece[q, :, 1152:1664]
    for q in range(4):
        gain[:, q * 1024 : q * 1024 + 1024] = inner[q : q + 1, 8192:9216]
    into[...] = inner[:, 0:4096]
    onto[...] = inner[:, 4096:6144]
    back[...] = inner[:, 6144:8192]
    width[...] = outer[...]


def exchange(x, axis):
    return lax.all_to_all(x, axis, split_axis=0, concat_axis=0, tiled=True)


def copies(x, count):
    return jnp.broadcast_to(x[None], (count,) + x.shape)


SWAP = [(0, 1), (1, 0)]


def summed_over_core(keep, send):
    (mine,) = call(add_kernel, [(keep.shape, F32)], [keep, lax.ppermute(send, "core", SWAP)])
    return exchange(mine, "x")


def per_device(
    perturbed,
    control_token_states,
    owners,
    matched_control_row,
    cell_time_bins,
    frozen,
    section_norm_gain,
    adapter_into_rank,
    adapter_onto_hidden,
    adapter_hidden_to_rank,
    adapter_to_width,
):
    plane = lax.axis_index("pipe")
    position = lax.axis_index(DP)
    places = jnp.stack([plane, lax.axis_index("core")]).astype(jnp.int32)

    weights = lax.all_gather(frozen[0], DP, axis=0, tiled=True)

    names = owners[:, :, 0]
    same = (names[:, :, None] == names[:, None, :]) & jnp.tril(jnp.ones((64, 64), bool), -1)[None]
    rank = jnp.sum(same.astype(jnp.int32), axis=2)
    batch = jnp.arange(2, dtype=jnp.int32)[:, None]
    slot = (names * 8 + batch * 4 + rank).reshape(TOKENS)
    row = (batch * 64 + matched_control_row).reshape(TOKENS)
    chosen = slot[:, None] == jnp.arange(512, dtype=jnp.int32)[None, :]
    table = jnp.sum(jnp.where(chosen, row[:, None], 0), axis=0).reshape(64, 8)
    own_width = adapter_to_width[0]
    before = [lax.ppermute(own_width, "pipe", [(i, i + k) for i in range(SECTIONS - k)]) for k in (1, 2, 3)]
    asked, *before = lax.optimization_barrier((exchange(table, DP), *before))
    asked = asked.reshape(512)

    pool = control_token_states.reshape(TOKENS, WIDTH)
    quarter = lax.dynamic_slice_in_dim(pool, plane * 1024, 1024, axis=1)
    picked = nn((asked[:, None] == jnp.arange(TOKENS, dtype=jnp.int32)[None, :]).astype(BF16), quarter)
    arrived = exchange(picked.astype(BF16).reshape(64, 8, 1024), DP).reshape(512, 1024)
    own_quarter = nn(chosen.astype(BF16), arrived).astype(BF16)
    source = exchange(copies(own_quarter, SECTIONS), "pipe")

    cell = position // 32
    bins = jnp.where(cell == 0, cell_time_bins[:, 0], cell_time_bins[:, 1])
    t_val = (bins.astype(F32) + 0.5) / NBINS
    frequency = jnp.exp(-jnp.log(10000.0) * jnp.arange(WIDTH // 2, dtype=F32) / (WIDTH // 2))
    angles = (t_val * 1000.0)[:, None] * frequency[None, :]
    features = jnp.concatenate([jnp.sin(angles), jnp.cos(angles)], axis=1)
    target = perturbed.reshape(TOKENS, WIDTH)
    (x0,) = call(entry_kernel, [((TOKENS, WIDTH), BF16)], [t_val, source, target, features], smem=1)

    gain = section_norm_gain
    into = adapter_into_rank[0].T
    onto = adapter_onto_hidden[0]
    back = adapter_hidden_to_rank[0].T
    stream = ((TOKENS, WIDTH), BF16)
    down = [(i, i + 1) for i in range(SECTIONS - 1)]
    up = [(i + 1, i) for i in range(SECTIONS - 1)]

    (widths,) = call(widths_kernel, [((SECTIONS, RANK, WIDTH), BF16)], [places, own_width, *before], smem=1)
    (squeezed_out,) = call(
        forward_first_kernel,
        [((1, 64, 128), BF16)],
        [places, x0, gain, weights, into, onto, back],
        scratch=[((WIDTH, HIDDEN), BF16), stream, pltpu.SemaphoreType.DMA((8,))],
        smem=1,
        hbm=(3,),
        limit=36,
        cost=6,
    )
    turned = []
    for tick in range(1, SECTIONS):
        squeezed_in = lax.ppermute(squeezed_out, "pipe", down)
        rows = PARTS[tick - 1]
        turned += call(
            functools.partial(transpose_kernel, sum(PARTS[: tick - 1]), rows),
            [((HIDDEN, rows), BF16)],
            [weights, squeezed_out],
            cost=3,
        )
        squeezed_in, turned[-1] = lax.optimization_barrier((squeezed_in, turned[-1]))
        if tick < SECTIONS - 1:
            (squeezed_out,) = call(
                functools.partial(forward_kernel, tick),
                [((tick + 1, 64, 128), BF16)],
                [places, x0, squeezed_in, widths, gain, weights, into, onto, back],
                scratch=[stream, stream],
                smem=1,
                cost=6,
            )
    xs, normed, inverse, lowered, slope, hidden, squeezed, seed, projected = call(
        forward_last_kernel,
        [
            stream,
            stream,
            ((TOKENS, 1), F32),
            ((TOKENS, RANK), BF16),
            ((TOKENS, HIDDEN), F32),
            ((TOKENS, HIDDEN), BF16),
            ((TOKENS, RANK), BF16),
            stream,
            ((SECTIONS, TOKENS, RANK), F32),
        ],
        [places, x0, squeezed_in, widths, gain, weights, into, onto, back, own_width, source, target],
        smem=1,
        cost=8,
    )

    own, received = projected, projected
    arrivals = []

    def hand_down(tick, d_stream, arrived):
        (handed,) = call(
            functools.partial(hand_down_kernel, tick),
            [((64, WIDTH), BF16)],
            [places, seed, d_stream, *arrivals[-1:]],
            smem=1,
        )
        handed, arrived = lax.optimization_barrier((handed, arrived))
        arrivals.append(lax.ppermute(handed, "pipe", up))
        return arrived

    for tick in range(SECTIONS - 1):
        sent, own, d_stream = call(
            functools.partial(backward_kernel, tick),
            [((SECTIONS - 1 - tick, 64, 128), F32), ((TOKENS, RANK), F32), ((TOKENS, WIDTH), F32)],
            [places, own, received, back, slope, onto, *turned, into, xs, inverse, gain, widths],
            scratch=[((TOKENS, HIDDEN), BF16)],
            smem=1,
            cost=8,
        )
        received = hand_down(tick, d_stream, lax.ppermute(sent, "pipe", up))
    keep, send = call(
        backward_last_kernel,
        [((4, RANK, 1152), F32)] * 2,
        [places, own, received, back, slope, onto, *turned, into, xs, inverse, gain, normed, lowered, hidden],
        scratch=[((TOKENS, HIDDEN), BF16), ((1, WIDTH), F32), ((RANK, 9216), F32)],
        smem=1,
        cost=8,
    )
    arrivals[-1], keep = lax.optimization_barrier((arrivals[-1], keep))
    hand_down(SECTIONS - 1, d_stream, received)
    inner = summed_over_core(keep, send)
    arrivals[-1], inner = lax.optimization_barrier((arrivals[-1], inner))
    keep, send = call(
        outward_kernel,
        [((4, RANK, 512), F32)] * 2,
        [places, squeezed, seed, *arrivals],
        scratch=[((RANK, WIDTH), F32)],
        smem=1,
    )
    outer = summed_over_core(keep, send)
    (along_x,) = call(x_sum_kernel, [((RANK, 1664), F32)], [inner, outer])
    (along_z,) = call(z_sum_kernel, [((8, 8, 1664), F32)], [exchange(along_x.reshape(8, 8, 1664), "z")])
    rows = exchange(along_z, "z").reshape(RANK, 1664)
    half = exchange(call(repeat_kernel, [((4, RANK, 1664), F32)], [rows])[0], "x")
    g_gain, g_into, g_onto, g_back, g_width = call(
        outputs_kernel,
        [((1, WIDTH), F32), ((RANK, WIDTH), F32), ((RANK, HIDDEN), F32), ((RANK, HIDDEN), F32), ((RANK, WIDTH), F32)],
        [places, half, lax.ppermute(half, "core", SWAP)],
        scratch=[((RANK, 9216), F32), ((RANK, WIDTH), F32)],
        smem=1,
    )
    return g_gain, g_into.T[None], g_onto[None], g_back.T[None], g_width[None]


def solution(mesh):
    cells = Mesh(mesh.devices.reshape(8, 4, 2, 4), ("z", "x", "core", "pipe"))
    in_specs = (
        P(None, DP, None),
        P(None, DP, None),
        P(None, DP, None),
        P(None, DP),
        P(),
        P("pipe", DP, None),
        P("pipe", None),
        P("pipe", None, None),
        P("pipe", None, None),
        P("pipe", None, None),
        P("pipe", None, None),
    )
    out_specs = (
        P("pipe", None),
        P("pipe", None, None),
        P("pipe", None, None),
        P("pipe", None, None),
        P("pipe", None, None),
    )
    return jax.shard_map(per_device, mesh=cells, in_specs=in_specs, out_specs=out_specs, check_vma=False)
```

```python
import functools

import jax
import jax.numpy as jnp
from jax import lax
from jax.experimental import pallas as pl
from jax.experimental.pallas import tpu as pltpu
from jax.sharding import Mesh
from jax.sharding import PartitionSpec as P

NBINS = 1000
EPSILON = 1e-05
TOKENS = 128
WIDTH = 4096
HIDDEN = 2048
RANK = 64
SECTIONS = 4
WIDE = 512
NARROW = 256
DP = ("z", "x", "core")
F32 = jnp.float32
BF16 = jnp.bfloat16
VMEM = pl.BlockSpec(memory_space=pltpu.VMEM)
SMEM = pl.BlockSpec(memory_space=pltpu.SMEM)
HBM = pl.BlockSpec(memory_space=pltpu.HBM)
PARTS = (1536, 1536, 1024)


def nn(left, right):
    return jnp.dot(left, right, preferred_element_type=F32)


def nt(left, right):
    return lax.dot_general(left, right, (((1,), (1,)), ((), ())), preferred_element_type=F32)


def tn(left, right):
    return lax.dot_general(left, right, (((0,), (0,)), ((), ())), preferred_element_type=F32)


def packed(value):
    return jnp.concatenate([value[0:64], value[64:128]], axis=1)


def unpacked(value):
    return jnp.concatenate([value[:, 0:64], value[:, 64:128]], axis=0)


def call(kernel, outs, args, scratch=(), smem=0, hbm=(), limit=8, cost=1):
    specs = [SMEM if i < smem else HBM if i in hbm else VMEM for i in range(len(args))]
    out_shape = tuple(jax.ShapeDtypeStruct(s, d) for s, d in outs)
    return pl.pallas_call(
        kernel,
        in_specs=specs,
        out_specs=tuple(VMEM for _ in outs),
        out_shape=out_shape,
        scratch_shapes=[s if hasattr(s, "memory_space") else pltpu.VMEM(*s) for s in scratch],
        cost_estimate=pl.CostEstimate(
            flops=cost * 10**9, bytes_accessed=cost * 3 * 10**6, transcendentals=0
        ),
        compiler_params=pltpu.CompilerParams(vmem_limit_bytes=limit << 20),
    )(*args)


def blocks(total, size):
    return [slice(i, i + size) for i in range(0, total, size)]


def entry_kernel(time_ref, source_ref, target_ref, feature_ref, out_ref):
    for batch in range(2):
        rows = slice(batch * 64, batch * 64 + 64)
        t = time_ref[batch]
        for q in range(SECTIONS):
            cols = slice(q * 1024, q * 1024 + 1024)
            source = source_ref[q, rows, :].astype(F32)
            target = target_ref[rows, cols].astype(F32)
            feature = feature_ref[batch : batch + 1, cols]
            out_ref[rows, cols] = ((1.0 - t) * source + t * target + feature).astype(BF16)


def widths_kernel(plane, own, one, two, three, out):
    for j in range(SECTIONS):
        for cols in blocks(WIDTH, WIDE):
            value = jnp.where(plane[0] == j, own[:, cols].astype(F32), 0.0)
            for k, part in ((1, one), (2, two), (3, three)):
                value = jnp.where(plane[0] == j + k, part[:, cols].astype(F32), value)
            out[j, :, cols] = value.astype(BF16)


def forward_body(x0, squeezed_in, widths, gain, into, xs, normed):
    total = jnp.zeros((TOKENS, 1), F32)
    steps = [unpacked(step.astype(F32)).astype(BF16) for step in squeezed_in]
    for cols in blocks(WIDTH, WIDE):
        x = x0[:, cols].astype(F32)
        for j, step in enumerate(steps):
            x = (x + nn(step, widths[j, :, cols])).astype(BF16).astype(F32)
        if xs is not x0:
            xs[:, cols] = x.astype(BF16)
        total = total + jnp.sum(x * x, axis=1, keepdims=True)
    inverse = lax.rsqrt(total * (1.0 / WIDTH) + EPSILON)
    lowered = jnp.zeros((TOKENS, RANK), F32)
    for cols in blocks(WIDTH, WIDE):
        value = (xs[:, cols].astype(F32) * inverse * gain[:, cols]).astype(BF16)
        normed[:, cols] = value
        lowered = lowered + nt(value, into[:, cols])
    lowered = lowered.astype(BF16)
    return inverse, lowered


def forward_tail(plane, tick, squeezed_in, lowered, normed, frozen, onto, back, out, arrived):
    squeezed = jnp.zeros((TOKENS, RANK), F32)
    for i, cols in enumerate(blocks(HIDDEN, NARROW)):
        arrived(i)
        pre = nn(normed[...], frozen[:, cols]) + nn(lowered, onto[:, cols])
        hidden = (pre * jax.nn.sigmoid(pre)).astype(BF16)
        squeezed = squeezed + nt(hidden, back[:, cols])
    squeezed = packed(squeezed)
    for j in range(tick):
        out[j] = jnp.where(plane[0] == j, squeezed, squeezed_in[j].astype(F32)).astype(BF16)
    out[tick] = jnp.where(plane[0] == tick, squeezed, 0.0).astype(BF16)


def forward_first_kernel(plane, x0, gain, weights, into, onto, back, out, frozen, normed, sems):
    moves = [
        pltpu.make_async_copy(weights.at[:, cols], frozen.at[:, cols], sems.at[i])
        for i, cols in enumerate(blocks(HIDDEN, NARROW))
    ]
    for move in moves:
        move.start()
    _, lowered = forward_body(x0, [], None, gain, into, x0, normed)
    forward_tail(plane, 0, None, lowered, normed, frozen, onto, back, out, lambda i: moves[i].wait())


def forward_kernel(tick, plane, x0, squeezed_in, widths, gain, frozen, into, onto, back, out, xs, normed):
    _, lowered = forward_body(x0, [squeezed_in[j] for j in range(tick)], widths, gain, into, xs, normed)
    forward_tail(plane, tick, squeezed_in, lowered, normed, frozen, onto, back, out, lambda i: None)


def transpose_kernel(first, rows, frozen, after, out):
    for r in range(0, rows, 256):
        for cols in blocks(HIDDEN, WIDE):
            out[cols, r : r + 256] = frozen[first + r : first + r + 256, cols].T


def forward_last_kernel(
    plane, x0, squeezed_in, widths, gain, frozen, into, onto, back, own_width, source, target,
    xs, normed, inverse_out, lowered_out, slope, hidden_out, squeezed_out, seed, projected,
):
    steps = [squeezed_in[j] for j in range(SECTIONS - 1)]
    inverse, lowered = forward_body(x0, steps, widths, gain, into, xs, normed)
    inverse_out[...] = inverse
    lowered_out[...] = lowered
    squeezed = jnp.zeros((TOKENS, RANK), F32)
    for cols in blocks(HIDDEN, NARROW):
        pre = nn(normed[...], frozen[:, cols]) + nn(lowered, onto[:, cols])
        sigmoid = jax.nn.sigmoid(pre)
        hidden = (pre * sigmoid).astype(BF16)
        slope[:, cols] = sigmoid * (1.0 + pre * (1.0 - sigmoid))
        hidden_out[:, cols] = hidden
        squeezed = squeezed + nt(hidden, back[:, cols])
    squeezed = squeezed.astype(BF16)
    squeezed_out[...] = squeezed
    scale = 8192.0 ** (-0.5)
    sums = [jnp.zeros((TOKENS, RANK), F32) for _ in range(SECTIONS)]
    for i, cols in enumerate(blocks(WIDTH, WIDE)):
        prediction = (xs[:, cols].astype(F32) + nn(squeezed, own_width[:, cols])).astype(BF16).astype(F32)
        part = slice((i % 2) * WIDE, (i % 2) * WIDE + WIDE)
        velocity = target[:, cols].astype(F32) - source[i // 2, :, part].astype(F32)
        value = ((prediction - velocity) * scale).astype(BF16)
        seed[:, cols] = value
        for j in range(SECTIONS):
            sums[j] = sums[j] + nt(value, widths[j, :, cols])
    for j in range(SECTIONS):
        projected[j] = sums[j]


def backward_body(d_squeezed, back, slope, onto, turned, into, xs, inverse, gain, d_pre, d_unit, gain_out):
    d_lowered = jnp.zeros((TOKENS, RANK), F32)
    for cols in blocks(HIDDEN, NARROW):
        value = (nn(d_squeezed, back[:, cols]) * slope[:, cols]).astype(BF16)
        d_pre[:, cols] = value
        d_lowered = d_lowered + nt(value, onto[:, cols])
    d_lowered = d_lowered.astype(BF16)
    total = jnp.zeros((TOKENS, 1), F32)
    for i, cols in enumerate(blocks(WIDTH, WIDE)):
        at = (i % 3) * WIDE
        d_normed = nn(d_pre[...], turned[i // 3][:, at : at + WIDE]) + nn(d_lowered, into[:, cols])
        unit = xs[:, cols].astype(F32) * inverse[...]
        if gain_out is not None:
            gain_out[:, cols] = jnp.sum(d_normed * unit, axis=0, keepdims=True)
        else:
            value = d_normed * gain[:, cols]
            d_unit[:, cols] = value
            total = total + jnp.sum(value * unit, axis=1, keepdims=True)
    return d_lowered, total


def backward_kernel(
    tick, plane, own, received, back, slope, onto, turned_a, turned_b, turned_c, into, xs, inverse, gain, widths,
    out, own_out, d_stream, d_pre,
):
    count = SECTIONS - 1 - tick
    base = [received[j] if tick == 0 else unpacked(received[j]) for j in range(count + (tick > 0))]
    if tick:
        own_out[...] = jnp.where(plane[0] == count, base[count], own[...])
    else:
        own_out[...] = own[SECTIONS - 1]
    turned = (turned_a, turned_b, turned_c)
    _, total = backward_body(
        own_out[...].astype(BF16), back, slope, onto, turned, into, xs, inverse, gain, d_pre, d_stream, None
    )
    mean = total * (1.0 / WIDTH)
    sums = [base[j] for j in range(count)]
    for cols in blocks(WIDTH, WIDE):
        unit = xs[:, cols].astype(F32) * inverse[...]
        value = inverse[...] * (d_stream[:, cols] - unit * mean)
        d_stream[:, cols] = value
        narrow = value.astype(BF16)
        for j in range(count):
            sums[j] = sums[j] + nt(narrow, widths[j, :, cols])
    for j in range(count):
        out[j] = packed(sums[j])


def hand_down_kernel(tick, plane, seed, d_stream, *rest):
    out = rest[-1]
    rows = pl.ds(pl.multiple_of(jnp.clip(tick - (SECTIONS - 1 - plane[0]), 0, 1) * 64, 64), 64)
    for cols in blocks(WIDTH, WIDE):
        held = seed[rows, cols].astype(F32)
        if len(rest) == 2:
            held = jnp.where(plane[0] == SECTIONS - 1, held, rest[0][:, cols].astype(F32))
        out[:, cols] = (held + d_stream[rows, cols]).astype(BF16)


def cut(grads, core, keep, send):
    piece = grads.shape[1] // 8
    for q in range(4):
        keep[q] = grads[:, pl.ds(pl.multiple_of((core * 4 + q) * piece, 128), piece)]
        send[q] = grads[:, pl.ds(pl.multiple_of(((1 - core) * 4 + q) * piece, 128), piece)]


def backward_last_kernel(
    plane, own, received, back, slope, onto, turned_a, turned_b, turned_c, into, xs, inverse, gain, normed, lowered,
    hidden, keep, send, d_pre, gain_row, grads,
):
    d_squeezed = jnp.where(plane[0] == 0, unpacked(received[0]), own[...]).astype(BF16)
    turned = (turned_a, turned_b, turned_c)
    d_lowered, _ = backward_body(
        d_squeezed, back, slope, onto, turned, into, xs, inverse, gain, d_pre, None, gain_row
    )
    for cols in blocks(WIDTH, WIDE):
        grads[:, cols] = tn(d_lowered, normed[:, cols])
    for cols in blocks(HIDDEN, WIDE):
        grads[:, 4096 + cols.start : 4096 + cols.stop] = tn(lowered[...], d_pre[:, cols])
        grads[:, 6144 + cols.start : 6144 + cols.stop] = tn(d_squeezed, hidden[:, cols])
    grads[:, 8192:9216] = jnp.zeros((RANK, 1024), F32)
    for q in range(4):
        grads[q : q + 1, 8192:9216] = gain_row[:, q * 1024 : q * 1024 + 1024]
    cut(grads, plane[1], keep, send)


def outward_kernel(plane, squeezed, seed, first, second, third, fourth, keep, send, grads):
    index = plane[0]
    for cols in blocks(WIDTH, WIDE):
        early = jnp.where(index == 2, first[:, cols], jnp.where(index == 1, second[:, cols], third[:, cols]))
        early = jnp.where(index == 3, seed[0:64, cols], early)
        late = jnp.where(index == 3, seed[64:128, cols], fourth[:, cols])
        grads[:, cols] = tn(squeezed[0:64, :], early) + tn(squeezed[64:128, :], late)
    cut(grads, plane[1], keep, send)


def core_sum_kernel(inner, inner_other, outer, outer_other, out):
    for q in range(4):
        out[q, :, 0:1152] = inner[q] + inner_other[q]
        out[q, :, 1152:1664] = outer[q] + outer_other[q]


def x_sum_kernel(parts, out):
    out[...] = (parts[0] + parts[1]) + (parts[2] + parts[3])


def z_sum_kernel(parts, out):
    total = parts[0]
    for k in range(1, 8):
        total = total + parts[k]
    for k in range(8):
        out[k] = total


def repeat_kernel(rows, out):
    for q in range(4):
        out[q] = rows[...]


def outputs_kernel(plane, half, other, gain, into, onto, back, width, inner, outer):
    core = plane[1]
    for side, piece in ((core, half), (1 - core, other)):
        for q in range(4):
            inner[:, pl.ds(pl.multiple_of((side * 4 + q) * 1152, 128), 1152)] = piece[q, :, 0:1152]
            outer[:, pl.ds(pl.multiple_of((side * 4 + q) * 512, 128), 512)] = piece[q, :, 1152:1664]
    for q in range(4):
        gain[:, q * 1024 : q * 1024 + 1024] = inner[q : q + 1, 8192:9216]
    into[...] = inner[:, 0:4096]
    onto[...] = inner[:, 4096:6144]
    back[...] = inner[:, 6144:8192]
    width[...] = outer[...]


def exchange(x, axis):
    return lax.all_to_all(x, axis, split_axis=0, concat_axis=0, tiled=True)


def copies(x, count):
    return jnp.broadcast_to(x[None], (count,) + x.shape)


SWAP = [(0, 1), (1, 0)]


def per_device(
    perturbed,
    control_token_states,
    owners,
    matched_control_row,
    cell_time_bins,
    frozen,
    section_norm_gain,
    adapter_into_rank,
    adapter_onto_hidden,
    adapter_hidden_to_rank,
    adapter_to_width,
):
    plane = lax.axis_index("pipe")
    position = lax.axis_index(DP)
    places = jnp.stack([plane, lax.axis_index("core")]).astype(jnp.int32)

    weights = lax.all_gather(frozen[0], DP, axis=0, tiled=True)

    names = owners[:, :, 0]
    same = (names[:, :, None] == names[:, None, :]) & jnp.tril(jnp.ones((64, 64), bool), -1)[None]
    rank = jnp.sum(same.astype(jnp.int32), axis=2)
    batch = jnp.arange(2, dtype=jnp.int32)[:, None]
    slot = (names * 8 + batch * 4 + rank).reshape(TOKENS)
    row = (batch * 64 + matched_control_row).reshape(TOKENS)
    chosen = slot[:, None] == jnp.arange(512, dtype=jnp.int32)[None, :]
    table = jnp.sum(jnp.where(chosen, row[:, None], 0), axis=0).reshape(64, 8)
    own_width = adapter_to_width[0]
    before = [lax.ppermute(own_width, "pipe", [(i, i + k) for i in range(SECTIONS - k)]) for k in (1, 2, 3)]
    asked, *before = lax.optimization_barrier((exchange(table, DP), *before))
    asked = asked.reshape(512)

    pool = control_token_states.reshape(TOKENS, WIDTH)
    quarter = lax.dynamic_slice_in_dim(pool, plane * 1024, 1024, axis=1)
    picked = nn((asked[:, None] == jnp.arange(TOKENS, dtype=jnp.int32)[None, :]).astype(BF16), quarter)
    arrived = exchange(picked.astype(BF16).reshape(64, 8, 1024), DP).reshape(512, 1024)
    own_quarter = nn(chosen.astype(BF16), arrived).astype(BF16)
    source = exchange(copies(own_quarter, SECTIONS), "pipe")

    cell = position // 32
    bins = jnp.where(cell == 0, cell_time_bins[:, 0], cell_time_bins[:, 1])
    t_val = (bins.astype(F32) + 0.5) / NBINS
    frequency = jnp.exp(-jnp.log(10000.0) * jnp.arange(WIDTH // 2, dtype=F32) / (WIDTH // 2))
    angles = (t_val * 1000.0)[:, None] * frequency[None, :]
    features = jnp.concatenate([jnp.sin(angles), jnp.cos(angles)], axis=1)
    target = perturbed.reshape(TOKENS, WIDTH)
    (x0,) = call(entry_kernel, [((TOKENS, WIDTH), BF16)], [t_val, source, target, features], smem=1)

    gain = section_norm_gain
    into = adapter_into_rank[0].T
    onto = adapter_onto_hidden[0]
    back = adapter_hidden_to_rank[0].T
    stream = ((TOKENS, WIDTH), BF16)
    down = [(i, i + 1) for i in range(SECTIONS - 1)]
    up = [(i + 1, i) for i in range(SECTIONS - 1)]

    (widths,) = call(widths_kernel, [((SECTIONS, RANK, WIDTH), BF16)], [places, own_width, *before], smem=1)
    (squeezed_out,) = call(
        forward_first_kernel,
        [((1, 64, 128), BF16)],
        [places, x0, gain, weights, into, onto, back],
        scratch=[((WIDTH, HIDDEN), BF16), stream, pltpu.SemaphoreType.DMA((8,))],
        smem=1,
        hbm=(3,),
        limit=36,
        cost=6,
    )
    turned = []
    for tick in range(1, SECTIONS):
        squeezed_in = lax.ppermute(squeezed_out, "pipe", down)
        rows = PARTS[tick - 1]
        turned += call(
            functools.partial(transpose_kernel, sum(PARTS[: tick - 1]), rows),
            [((HIDDEN, rows), BF16)],
            [weights, squeezed_out],
            cost=3,
        )
        squeezed_in, turned[-1] = lax.optimization_barrier((squeezed_in, turned[-1]))
        if tick < SECTIONS - 1:
            (squeezed_out,) = call(
                functools.partial(forward_kernel, tick),
                [((tick + 1, 64, 128), BF16)],
                [places, x0, squeezed_in, widths, gain, weights, into, onto, back],
                scratch=[stream, stream],
                smem=1,
                cost=6,
            )
    xs, normed, inverse, lowered, slope, hidden, squeezed, seed, projected = call(
        forward_last_kernel,
        [
            stream,
            stream,
            ((TOKENS, 1), F32),
            ((TOKENS, RANK), BF16),
            ((TOKENS, HIDDEN), F32),
            ((TOKENS, HIDDEN), BF16),
            ((TOKENS, RANK), BF16),
            stream,
            ((SECTIONS, TOKENS, RANK), F32),
        ],
        [places, x0, squeezed_in, widths, gain, weights, into, onto, back, own_width, source, target],
        smem=1,
        cost=8,
    )

    own, received = projected, projected
    arrivals = []

    def hand_down(tick, d_stream, arrived):
        (handed,) = call(
            functools.partial(hand_down_kernel, tick),
            [((64, WIDTH), BF16)],
            [places, seed, d_stream, *arrivals[-1:]],
            smem=1,
        )
        handed, arrived = lax.optimization_barrier((handed, arrived))
        arrivals.append(lax.ppermute(handed, "pipe", up))
        return arrived

    for tick in range(SECTIONS - 1):
        sent, own, d_stream = call(
            functools.partial(backward_kernel, tick),
            [((SECTIONS - 1 - tick, 64, 128), F32), ((TOKENS, RANK), F32), ((TOKENS, WIDTH), F32)],
            [places, own, received, back, slope, onto, *turned, into, xs, inverse, gain, widths],
            scratch=[((TOKENS, HIDDEN), BF16)],
            smem=1,
            cost=8,
        )
        received = hand_down(tick, d_stream, lax.ppermute(sent, "pipe", up))
    keep, send = call(
        backward_last_kernel,
        [((4, RANK, 1152), F32)] * 2,
        [places, own, received, back, slope, onto, *turned, into, xs, inverse, gain, normed, lowered, hidden],
        scratch=[((TOKENS, HIDDEN), BF16), ((1, WIDTH), F32), ((RANK, 9216), F32)],
        smem=1,
        cost=8,
    )
    arrivals[-1], keep = lax.optimization_barrier((arrivals[-1], keep))
    hand_down(SECTIONS - 1, d_stream, received)
    inner = [keep, lax.ppermute(send, "core", SWAP)]
    keep, send = call(
        outward_kernel,
        [((4, RANK, 512), F32)] * 2,
        [places, squeezed, seed, *arrivals],
        scratch=[((RANK, WIDTH), F32)],
        smem=1,
    )
    (mine,) = call(core_sum_kernel, [((4, RANK, 1664), F32)], [*inner, keep, lax.ppermute(send, "core", SWAP)])
    (along_x,) = call(x_sum_kernel, [((RANK, 1664), F32)], [exchange(mine, "x")])
    (along_z,) = call(z_sum_kernel, [((8, 8, 1664), F32)], [exchange(along_x.reshape(8, 8, 1664), "z")])
    rows = exchange(along_z, "z").reshape(RANK, 1664)
    half = exchange(call(repeat_kernel, [((4, RANK, 1664), F32)], [rows])[0], "x")
    g_gain, g_into, g_onto, g_back, g_width = call(
        outputs_kernel,
        [((1, WIDTH), F32), ((RANK, WIDTH), F32), ((RANK, HIDDEN), F32), ((RANK, HIDDEN), F32), ((RANK, WIDTH), F32)],
        [places, half, lax.ppermute(half, "core", SWAP)],
        scratch=[((RANK, 9216), F32), ((RANK, WIDTH), F32)],
        smem=1,
    )
    return g_gain, g_into.T[None], g_onto[None], g_back.T[None], g_width[None]


def solution(mesh):
    cells = Mesh(mesh.devices.reshape(8, 4, 2, 4), ("z", "x", "core", "pipe"))
    in_specs = (
        P(None, DP, None),
        P(None, DP, None),
        P(None, DP, None),
        P(None, DP),
        P(),
        P("pipe", DP, None),
        P("pipe", None),
        P("pipe", None, None),
        P("pipe", None, None),
        P("pipe", None, None),
        P("pipe", None, None),
    )
    out_specs = (
        P("pipe", None),
        P("pipe", None, None),
        P("pipe", None, None),
        P("pipe", None, None),
        P("pipe", None, None),
    )
    return jax.shard_map(per_device, mesh=cells, in_specs=in_specs, out_specs=out_specs, check_vma=False)
```

```python
import functools

import jax
import jax.numpy as jnp
from jax import lax
from jax.experimental import pallas as pl
from jax.experimental.pallas import tpu as pltpu
from jax.sharding import Mesh
from jax.sharding import PartitionSpec as P

NBINS = 1000
EPSILON = 1e-05
TOKENS = 128
WIDTH = 4096
HIDDEN = 2048
RANK = 64
SECTIONS = 4
WIDE = 512
NARROW = 256
DP = ("z", "x", "core")
F32 = jnp.float32
BF16 = jnp.bfloat16
VMEM = pl.BlockSpec(memory_space=pltpu.VMEM)
SMEM = pl.BlockSpec(memory_space=pltpu.SMEM)
HBM = pl.BlockSpec(memory_space=pltpu.HBM)
PARTS = (1536, 1536, 1024)


def nn(left, right):
    return jnp.dot(left, right, preferred_element_type=F32)


def nt(left, right):
    return lax.dot_general(left, right, (((1,), (1,)), ((), ())), preferred_element_type=F32)


def tn(left, right):
    return lax.dot_general(left, right, (((0,), (0,)), ((), ())), preferred_element_type=F32)


def packed(value):
    return jnp.concatenate([value[0:64], value[64:128]], axis=1)


def unpacked(value):
    return jnp.concatenate([value[:, 0:64], value[:, 64:128]], axis=0)


def call(kernel, outs, args, scratch=(), smem=0, hbm=(), limit=8, cost=1):
    specs = [SMEM if i < smem else HBM if i in hbm else VMEM for i in range(len(args))]
    out_shape = tuple(jax.ShapeDtypeStruct(s, d) for s, d in outs)
    return pl.pallas_call(
        kernel,
        in_specs=specs,
        out_specs=tuple(VMEM for _ in outs),
        out_shape=out_shape,
        scratch_shapes=[s if hasattr(s, "memory_space") else pltpu.VMEM(*s) for s in scratch],
        cost_estimate=pl.CostEstimate(
            flops=cost * 10**9, bytes_accessed=cost * 3 * 10**6, transcendentals=0
        ),
        compiler_params=pltpu.CompilerParams(vmem_limit_bytes=limit << 20),
    )(*args)


def blocks(total, size):
    return [slice(i, i + size) for i in range(0, total, size)]


def entry_kernel(time_ref, source_ref, target_ref, feature_ref, out_ref):
    for batch in range(2):
        rows = slice(batch * 64, batch * 64 + 64)
        t = time_ref[batch]
        for q in range(SECTIONS):
            cols = slice(q * 1024, q * 1024 + 1024)
            source = source_ref[q, rows, :].astype(F32)
            target = target_ref[rows, cols].astype(F32)
            feature = feature_ref[batch : batch + 1, cols]
            out_ref[rows, cols] = ((1.0 - t) * source + t * target + feature).astype(BF16)


def widths_kernel(plane, own, one, two, three, out):
    for j in range(SECTIONS):
        for cols in blocks(WIDTH, WIDE):
            value = jnp.where(plane[0] == j, own[:, cols].astype(F32), 0.0)
            for k, part in ((1, one), (2, two), (3, three)):
                value = jnp.where(plane[0] == j + k, part[:, cols].astype(F32), value)
            out[j, :, cols] = value.astype(BF16)


def forward_body(plane, x0, squeezed_in, widths, gain, into, xs, normed):
    total = jnp.zeros((TOKENS, 1), F32)
    steps = [
        jnp.where(plane[0] > j, unpacked(step.astype(F32)), 0.0).astype(BF16) for j, step in enumerate(squeezed_in)
    ]
    for cols in blocks(WIDTH, WIDE):
        x = x0[:, cols].astype(F32)
        for j, step in enumerate(steps):
            x = (x + nn(step, widths[j, :, cols])).astype(BF16).astype(F32)
        if xs is not x0:
            xs[:, cols] = x.astype(BF16)
        total = total + jnp.sum(x * x, axis=1, keepdims=True)
    inverse = lax.rsqrt(total * (1.0 / WIDTH) + EPSILON)
    lowered = jnp.zeros((TOKENS, RANK), F32)
    for cols in blocks(WIDTH, WIDE):
        value = (xs[:, cols].astype(F32) * inverse * gain[:, cols]).astype(BF16)
        normed[:, cols] = value
        lowered = lowered + nt(value, into[:, cols])
    lowered = lowered.astype(BF16)
    return inverse, lowered


def forward_tail(plane, tick, squeezed_in, lowered, normed, frozen, onto, back, out, arrived):
    squeezed = jnp.zeros((TOKENS, RANK), F32)
    for i, cols in enumerate(blocks(HIDDEN, NARROW)):
        arrived(i)
        pre = nn(normed[...], frozen[:, cols]) + nn(lowered, onto[:, cols])
        hidden = (pre * jax.nn.sigmoid(pre)).astype(BF16)
        squeezed = squeezed + nt(hidden, back[:, cols])
    squeezed = packed(squeezed)
    for j in range(tick):
        out[j] = jnp.where(plane[0] == j, squeezed, squeezed_in[j].astype(F32)).astype(BF16)
    out[tick] = jnp.where(plane[0] == tick, squeezed, 0.0).astype(BF16)


def forward_first_kernel(plane, x0, gain, weights, into, onto, back, out, frozen, normed, sems):
    moves = [
        pltpu.make_async_copy(weights.at[:, cols], frozen.at[:, cols], sems.at[i])
        for i, cols in enumerate(blocks(HIDDEN, NARROW))
    ]
    for move in moves:
        move.start()
    _, lowered = forward_body(plane, x0, [], None, gain, into, x0, normed)
    forward_tail(plane, 0, None, lowered, normed, frozen, onto, back, out, lambda i: moves[i].wait())


def forward_kernel(tick, plane, x0, squeezed_in, widths, gain, frozen, into, onto, back, out, xs, normed):
    _, lowered = forward_body(plane, x0, [squeezed_in[j] for j in range(tick)], widths, gain, into, xs, normed)
    forward_tail(plane, tick, squeezed_in, lowered, normed, frozen, onto, back, out, lambda i: None)


def transpose_kernel(first, rows, frozen, after, out):
    for r in range(0, rows, 256):
        for cols in blocks(HIDDEN, WIDE):
            out[cols, r : r + 256] = frozen[first + r : first + r + 256, cols].T


def forward_last_kernel(
    plane, x0, squeezed_in, widths, gain, frozen, into, onto, back, own_width, source, target,
    xs, normed, inverse_out, lowered_out, slope, hidden_out, squeezed_out, seed, projected,
):
    steps = [squeezed_in[j] for j in range(SECTIONS - 1)]
    inverse, lowered = forward_body(plane, x0, steps, widths, gain, into, xs, normed)
    inverse_out[...] = inverse
    lowered_out[...] = lowered
    squeezed = jnp.zeros((TOKENS, RANK), F32)
    for cols in blocks(HIDDEN, NARROW):
        pre = nn(normed[...], frozen[:, cols]) + nn(lowered, onto[:, cols])
        sigmoid = jax.nn.sigmoid(pre)
        hidden = (pre * sigmoid).astype(BF16)
        slope[:, cols] = sigmoid * (1.0 + pre * (1.0 - sigmoid))
        hidden_out[:, cols] = hidden
        squeezed = squeezed + nt(hidden, back[:, cols])
    squeezed = squeezed.astype(BF16)
    squeezed_out[...] = squeezed
    scale = 8192.0 ** (-0.5)
    total = jnp.zeros((TOKENS, RANK), F32)
    for i, cols in enumerate(blocks(WIDTH, WIDE)):
        prediction = (xs[:, cols].astype(F32) + nn(squeezed, own_width[:, cols])).astype(BF16).astype(F32)
        part = slice((i % 2) * WIDE, (i % 2) * WIDE + WIDE)
        velocity = target[:, cols].astype(F32) - source[i // 2, :, part].astype(F32)
        value = ((prediction - velocity) * scale).astype(BF16)
        seed[:, cols] = value
        total = total + nt(value, own_width[:, cols])
    projected[...] = total


def backward_body(d_squeezed, back, slope, onto, turned, into, xs, inverse, gain, d_pre, d_unit, gain_out):
    d_lowered = jnp.zeros((TOKENS, RANK), F32)
    for cols in blocks(HIDDEN, NARROW):
        value = (nn(d_squeezed, back[:, cols]) * slope[:, cols]).astype(BF16)
        d_pre[:, cols] = value
        d_lowered = d_lowered + nt(value, onto[:, cols])
    d_lowered = d_lowered.astype(BF16)
    total = jnp.zeros((TOKENS, 1), F32)
    for i, cols in enumerate(blocks(WIDTH, WIDE)):
        at = (i % 3) * WIDE
        d_normed = nn(d_pre[...], turned[i // 3][:, at : at + WIDE]) + nn(d_lowered, into[:, cols])
        unit = xs[:, cols].astype(F32) * inverse[...]
        if gain_out is not None:
            gain_out[:, cols] = jnp.sum(d_normed * unit, axis=0, keepdims=True)
        else:
            value = d_normed * gain[:, cols]
            d_unit[:, cols] = value
            total = total + jnp.sum(value * unit, axis=1, keepdims=True)
    return d_lowered, total


def backward_kernel(
    tick, plane, own, received, back, slope, onto, turned_a, turned_b, turned_c, into, xs, inverse, gain, widths,
    out, own_out, d_stream, d_pre,
):
    count = SECTIONS - 1 - tick
    if tick:
        base = [unpacked(received[j]) for j in range(count + 1)]
        own_out[...] = jnp.where(plane[0] == count, base[count], own[...])
    else:
        base = [jnp.zeros((TOKENS, RANK), F32)] * count
        own_out[...] = own[...]
    turned = (turned_a, turned_b, turned_c)
    _, total = backward_body(
        own_out[...].astype(BF16), back, slope, onto, turned, into, xs, inverse, gain, d_pre, d_stream, None
    )
    mean = total * (1.0 / WIDTH)
    sums = [base[j] for j in range(count)]
    for cols in blocks(WIDTH, WIDE):
        unit = xs[:, cols].astype(F32) * inverse[...]
        value = inverse[...] * (d_stream[:, cols] - unit * mean)
        d_stream[:, cols] = value
        if tick == 0:
            value = received[:, cols].astype(F32) + value
        narrow = value.astype(BF16)
        for j in range(count):
            sums[j] = sums[j] + nt(narrow, widths[j, :, cols])
    for j in range(count):
        out[j] = packed(sums[j])


def hand_down_kernel(tick, plane, seed, d_stream, *rest):
    out = rest[-1]
    rows = pl.ds(pl.multiple_of(jnp.clip(tick - (SECTIONS - 1 - plane[0]), 0, 1) * 64, 64), 64)
    for cols in blocks(WIDTH, WIDE):
        held = seed[rows, cols].astype(F32)
        if len(rest) == 2:
            held = jnp.where(plane[0] == SECTIONS - 1, held, rest[0][:, cols].astype(F32))
        out[:, cols] = (held + d_stream[rows, cols]).astype(BF16)


def cut(grads, core, keep, send):
    piece = grads.shape[1] // 8
    for q in range(4):
        keep[q] = grads[:, pl.ds(pl.multiple_of((core * 4 + q) * piece, 128), piece)]
        send[q] = grads[:, pl.ds(pl.multiple_of(((1 - core) * 4 + q) * piece, 128), piece)]


def backward_last_kernel(
    plane, own, received, back, slope, onto, turned_a, turned_b, turned_c, into, xs, inverse, gain, normed, lowered,
    hidden, keep, send, d_pre, gain_row, grads,
):
    d_squeezed = jnp.where(plane[0] == 0, unpacked(received[0]), own[...]).astype(BF16)
    turned = (turned_a, turned_b, turned_c)
    d_lowered, _ = backward_body(
        d_squeezed, back, slope, onto, turned, into, xs, inverse, gain, d_pre, None, gain_row
    )
    for cols in blocks(WIDTH, WIDE):
        grads[:, cols] = tn(d_lowered, normed[:, cols])
    for cols in blocks(HIDDEN, WIDE):
        grads[:, 4096 + cols.start : 4096 + cols.stop] = tn(lowered[...], d_pre[:, cols])
        grads[:, 6144 + cols.start : 6144 + cols.stop] = tn(d_squeezed, hidden[:, cols])
    grads[:, 8192:9216] = jnp.zeros((RANK, 1024), F32)
    for q in range(4):
        grads[q : q + 1, 8192:9216] = gain_row[:, q * 1024 : q * 1024 + 1024]
    cut(grads, plane[1], keep, send)


def outward_kernel(plane, squeezed, seed, first, second, third, fourth, keep, send, grads):
    index = plane[0]
    for cols in blocks(WIDTH, WIDE):
        early = jnp.where(index == 2, first[:, cols], jnp.where(index == 1, second[:, cols], third[:, cols]))
        early = jnp.where(index == 3, seed[0:64, cols], early)
        late = jnp.where(index == 3, seed[64:128, cols], fourth[:, cols])
        grads[:, cols] = tn(squeezed[0:64, :], early) + tn(squeezed[64:128, :], late)
    cut(grads, plane[1], keep, send)


def core_sum_kernel(plane, inner, inner_other, outer, outer_other, top, bottom, own, right, left):
    for k, outs in ((2, (top, bottom)), (1, (right,)), (3, (left,)), (0, (own,))):
        q = lax.rem(plane[2] + k, 4)
        for half, out in enumerate(outs):
            rows = slice(half * 32, half * 32 + 64 // len(outs))
            out[:, 0:1152] = inner[q, rows, :] + inner_other[q, rows, :]
            out[:, 1152:1664] = outer[q, rows, :] + outer_other[q, rows, :]


def add_rows_kernel(right, top, left, bottom, right_out, left_out):
    right_out[0:32, :] = right[0:32, :] + top[...]
    right_out[32:64, :] = right[32:64, :]
    left_out[0:32, :] = left[0:32, :]
    left_out[32:64, :] = left[32:64, :] + bottom[...]


def x_sum_kernel(own, first, second, out):
    out[...] = (own[...] + first[...]) + second[...]


def z_sum_kernel(parts, out):
    total = parts[0]
    for k in range(1, 8):
        total = total + parts[k]
    for k in range(8):
        out[k] = total


def outputs_kernel(plane, *refs):
    pieces, others, (gain, into, onto, back, width, inner, outer) = refs[0:5], refs[5:10], refs[10:]
    for side, group in ((plane[1], pieces), (1 - plane[1], others)):
        for k, first, piece in zip((0, 3, 1, 2, 2), (0, 0, 0, 0, 32), group):
            q = side * 4 + lax.rem(plane[2] + k, 4)
            rows = slice(first, first + piece.shape[0])
            inner[rows, pl.ds(pl.multiple_of(q * 1152, 128), 1152)] = piece[:, 0:1152]
            outer[rows, pl.ds(pl.multiple_of(q * 512, 128), 512)] = piece[:, 1152:1664]
    for q in range(4):
        gain[:, q * 1024 : q * 1024 + 1024] = inner[q : q + 1, 8192:9216]
    into[...] = inner[:, 0:4096]
    onto[...] = inner[:, 4096:6144]
    back[...] = inner[:, 6144:8192]
    width[...] = outer[...]


def exchange(x, axis):
    return lax.all_to_all(x, axis, split_axis=0, concat_axis=0, tiled=True)


def copies(x, count):
    return jnp.broadcast_to(x[None], (count,) + x.shape)


SWAP = [(0, 1), (1, 0)]


def rightward(x):
    return lax.ppermute(x, "x", [(i, (i + 1) % 4) for i in range(4)])


def leftward(x):
    return lax.ppermute(x, "x", [((i + 1) % 4, i) for i in range(4)])


def per_device(
    perturbed,
    control_token_states,
    owners,
    matched_control_row,
    cell_time_bins,
    frozen,
    section_norm_gain,
    adapter_into_rank,
    adapter_onto_hidden,
    adapter_hidden_to_rank,
    adapter_to_width,
):
    plane = lax.axis_index("pipe")
    position = lax.axis_index(DP)
    places = jnp.stack([plane, lax.axis_index("core"), lax.axis_index("x")]).astype(jnp.int32)

    weights = lax.all_gather(frozen[0], DP, axis=0, tiled=True)

    names = owners[:, :, 0]
    same = (names[:, :, None] == names[:, None, :]) & jnp.tril(jnp.ones((64, 64), bool), -1)[None]
    rank = jnp.sum(same.astype(jnp.int32), axis=2)
    batch = jnp.arange(2, dtype=jnp.int32)[:, None]
    slot = (names * 8 + batch * 4 + rank).reshape(TOKENS)
    row = (batch * 64 + matched_control_row).reshape(TOKENS)
    chosen = slot[:, None] == jnp.arange(512, dtype=jnp.int32)[None, :]
    table = jnp.sum(jnp.where(chosen, row[:, None], 0), axis=0).reshape(64, 8)
    own_width = adapter_to_width[0]
    before = [lax.ppermute(own_width, "pipe", [(i, i + k) for i in range(SECTIONS - k)]) for k in (1, 2, 3)]
    asked, *before = lax.optimization_barrier((exchange(table, DP), *before))
    asked = asked.reshape(512)

    pool = control_token_states.reshape(TOKENS, WIDTH)
    quarter = lax.dynamic_slice_in_dim(pool, plane * 1024, 1024, axis=1)
    picked = nn((asked[:, None] == jnp.arange(TOKENS, dtype=jnp.int32)[None, :]).astype(BF16), quarter)
    arrived = exchange(picked.astype(BF16).reshape(64, 8, 1024), DP).reshape(512, 1024)
    own_quarter = nn(chosen.astype(BF16), arrived).astype(BF16)
    source = exchange(copies(own_quarter, SECTIONS), "pipe")

    cell = position // 32
    bins = jnp.where(cell == 0, cell_time_bins[:, 0], cell_time_bins[:, 1])
    t_val = (bins.astype(F32) + 0.5) / NBINS
    frequency = jnp.exp(-jnp.log(10000.0) * jnp.arange(WIDTH // 2, dtype=F32) / (WIDTH // 2))
    angles = (t_val * 1000.0)[:, None] * frequency[None, :]
    features = jnp.concatenate([jnp.sin(angles), jnp.cos(angles)], axis=1)
    target = perturbed.reshape(TOKENS, WIDTH)
    (x0,) = call(entry_kernel, [((TOKENS, WIDTH), BF16)], [t_val, source, target, features], smem=1)

    gain = section_norm_gain
    into = adapter_into_rank[0].T
    onto = adapter_onto_hidden[0]
    back = adapter_hidden_to_rank[0].T
    stream = ((TOKENS, WIDTH), BF16)
    down = [(i, (i + 1) % SECTIONS) for i in range(SECTIONS)]
    up = [((i + 1) % SECTIONS, i) for i in range(SECTIONS)]

    (widths,) = call(widths_kernel, [((SECTIONS, RANK, WIDTH), BF16)], [places, own_width, *before], smem=1)
    (squeezed_out,) = call(
        forward_first_kernel,
        [((1, 64, 128), BF16)],
        [places, x0, gain, weights, into, onto, back],
        scratch=[((WIDTH, HIDDEN), BF16), stream, pltpu.SemaphoreType.DMA((8,))],
        smem=1,
        hbm=(3,),
        limit=36,
        cost=6,
    )
    turned = []
    for tick in range(1, SECTIONS):
        squeezed_in = lax.ppermute(squeezed_out, "pipe", down)
        rows = PARTS[tick - 1]
        turned += call(
            functools.partial(transpose_kernel, sum(PARTS[: tick - 1]), rows),
            [((HIDDEN, rows), BF16)],
            [weights, squeezed_out],
            cost=3,
        )
        squeezed_in, turned[-1] = lax.optimization_barrier((squeezed_in, turned[-1]))
        if tick < SECTIONS - 1:
            (squeezed_out,) = call(
                functools.partial(forward_kernel, tick),
                [((tick + 1, 64, 128), BF16)],
                [places, x0, squeezed_in, widths, gain, weights, into, onto, back],
                scratch=[stream, stream],
                smem=1,
                cost=6,
            )
    xs, normed, inverse, lowered, slope, hidden, squeezed, seed, projected = call(
        forward_last_kernel,
        [
            stream,
            stream,
            ((TOKENS, 1), F32),
            ((TOKENS, RANK), BF16),
            ((TOKENS, HIDDEN), F32),
            ((TOKENS, HIDDEN), BF16),
            ((TOKENS, RANK), BF16),
            stream,
            ((TOKENS, RANK), F32),
        ],
        [places, x0, squeezed_in, widths, gain, weights, into, onto, back, own_width, source, target],
        smem=1,
        cost=8,
    )

    own, received = projected, seed
    arrivals = []

    def hand_down(tick, d_stream, arrived):
        (handed,) = call(
            functools.partial(hand_down_kernel, tick),
            [((64, WIDTH), BF16)],
            [places, seed, d_stream, *arrivals[-1:]],
            smem=1,
        )
        handed, arrived = lax.optimization_barrier((handed, arrived))
        arrivals.append(lax.ppermute(handed, "pipe", up))
        return arrived

    for tick in range(SECTIONS - 1):
        sent, own, d_stream = call(
            functools.partial(backward_kernel, tick),
            [((SECTIONS - 1 - tick, 64, 128), F32), ((TOKENS, RANK), F32), ((TOKENS, WIDTH), F32)],
            [places, own, received, back, slope, onto, *turned, into, xs, inverse, gain, widths],
            scratch=[((TOKENS, HIDDEN), BF16)],
            smem=1,
            cost=8,
        )
        received = hand_down(tick, d_stream, lax.ppermute(sent, "pipe", up))
    keep, send = call(
        backward_last_kernel,
        [((4, RANK, 1152), F32)] * 2,
        [places, own, received, back, slope, onto, *turned, into, xs, inverse, gain, normed, lowered, hidden],
        scratch=[((TOKENS, HIDDEN), BF16), ((1, WIDTH), F32), ((RANK, 9216), F32)],
        smem=1,
        cost=8,
    )
    arrivals[-1], keep = lax.optimization_barrier((arrivals[-1], keep))
    hand_down(SECTIONS - 1, d_stream, received)
    inner = [keep, lax.ppermute(send, "core", SWAP)]
    keep, send = call(
        outward_kernel,
        [((4, RANK, 512), F32)] * 2,
        [places, squeezed, seed, *arrivals],
        scratch=[((RANK, WIDTH), F32)],
        smem=1,
    )
    piece, part = ((RANK, 1664), F32), ((RANK // 2, 1664), F32)
    top, bottom, own_piece, right, left = call(
        core_sum_kernel,
        [part, part, piece, piece, piece],
        [places, *inner, keep, lax.ppermute(send, "core", SWAP)],
        smem=1,
    )
    right, left = call(add_rows_kernel, [piece, piece], [right, rightward(top), left, leftward(bottom)])
    (along_x,) = call(x_sum_kernel, [piece], [own_piece, rightward(right), leftward(left)])
    (along_z,) = call(z_sum_kernel, [((8, 8, 1664), F32)], [exchange(along_x.reshape(8, 8, 1664), "z")])
    rows = exchange(along_z, "z").reshape(RANK, 1664)
    before, after = rightward(rows), leftward(rows)
    pieces = [rows, before, after, rightward(before[0:32]), leftward(after[32:64])]
    others = [lax.ppermute(p, "core", SWAP) for p in pieces]
    g_gain, g_into, g_onto, g_back, g_width = call(
        outputs_kernel,
        [((1, WIDTH), F32), ((RANK, WIDTH), F32), ((RANK, HIDDEN), F32), ((RANK, HIDDEN), F32), ((RANK, WIDTH), F32)],
        [places, *pieces, *others],
        scratch=[((RANK, 9216), F32), ((RANK, WIDTH), F32)],
        smem=1,
    )
    return g_gain, g_into.T[None], g_onto[None], g_back.T[None], g_width[None]


def solution(mesh):
    cells = Mesh(mesh.devices.reshape(8, 4, 2, 4), ("z", "x", "core", "pipe"))
    in_specs = (
        P(None, DP, None),
        P(None, DP, None),
        P(None, DP, None),
        P(None, DP),
        P(),
        P("pipe", DP, None),
        P("pipe", None),
        P("pipe", None, None),
        P("pipe", None, None),
        P("pipe", None, None),
        P("pipe", None, None),
    )
    out_specs = (
        P("pipe", None),
        P("pipe", None, None),
        P("pipe", None, None),
        P("pipe", None, None),
        P("pipe", None, None),
    )
    return jax.shard_map(per_device, mesh=cells, in_specs=in_specs, out_specs=out_specs, check_vma=False)
```

```python
import functools

import jax
import jax.numpy as jnp
from jax import lax
from jax.experimental import pallas as pl
from jax.experimental.pallas import tpu as pltpu
from jax.sharding import Mesh
from jax.sharding import PartitionSpec as P

NBINS = 1000
EPSILON = 1e-05
TOKENS = 128
WIDTH = 4096
HIDDEN = 2048
RANK = 64
SECTIONS = 4
WIDE = 512
NARROW = 256
DP = ("z", "x", "core")
F32 = jnp.float32
BF16 = jnp.bfloat16
VMEM = pl.BlockSpec(memory_space=pltpu.VMEM)
SMEM = pl.BlockSpec(memory_space=pltpu.SMEM)
HBM = pl.BlockSpec(memory_space=pltpu.HBM)
PARTS = (1536, 1536, 1024)


def nn(left, right):
    return jnp.dot(left, right, preferred_element_type=F32)


def nt(left, right):
    return lax.dot_general(left, right, (((1,), (1,)), ((), ())), preferred_element_type=F32)


def tn(left, right):
    return lax.dot_general(left, right, (((0,), (0,)), ((), ())), preferred_element_type=F32)


def packed(value):
    return jnp.concatenate([value[0:64], value[64:128]], axis=1)


def unpacked(value):
    return jnp.concatenate([value[:, 0:64], value[:, 64:128]], axis=0)


def call(kernel, outs, args, scratch=(), smem=0, hbm=(), limit=8, cost=1):
    specs = [SMEM if i < smem else HBM if i in hbm else VMEM for i in range(len(args))]
    out_shape = tuple(jax.ShapeDtypeStruct(s, d) for s, d in outs)
    return pl.pallas_call(
        kernel,
        in_specs=specs,
        out_specs=tuple(VMEM for _ in outs),
        out_shape=out_shape,
        scratch_shapes=[s if hasattr(s, "memory_space") else pltpu.VMEM(*s) for s in scratch],
        cost_estimate=pl.CostEstimate(
            flops=cost * 10**9, bytes_accessed=cost * 3 * 10**6, transcendentals=0
        ),
        compiler_params=pltpu.CompilerParams(vmem_limit_bytes=limit << 20),
    )(*args)


def blocks(total, size):
    return [slice(i, i + size) for i in range(0, total, size)]


def entry_kernel(time_ref, source_ref, target_ref, feature_ref, into, onto, back, out_ref, joined):
    for batch in range(2):
        rows = slice(batch * 64, batch * 64 + 64)
        t = time_ref[batch]
        for q in range(SECTIONS):
            cols = slice(q * 1024, q * 1024 + 1024)
            source = source_ref[q, rows, :].astype(F32)
            target = target_ref[rows, cols].astype(F32)
            feature = feature_ref[batch : batch + 1, cols]
            value = ((1.0 - t) * source + t * target + feature).astype(BF16)
            out_ref[rows, cols] = value
            joined[rows, cols] = value
    joined[128:192, :] = into[...]
    joined[192:256, 0:2048] = onto[...]
    joined[192:256, 2048:4096] = back[...]


def widths_kernel(plane, own, one, two, three, out):
    for j in range(SECTIONS):
        for cols in blocks(WIDTH, WIDE):
            value = jnp.where(plane[0] == j, own[:, cols].astype(F32), 0.0)
            for k, part in ((1, one), (2, two), (3, three)):
                value = jnp.where(plane[0] == j + k, part[:, cols].astype(F32), value)
            out[j, :, cols] = value.astype(BF16)


def forward_body(plane, x0, squeezed_in, widths, gain, into, xs, normed):
    total = jnp.zeros((TOKENS, 1), F32)
    steps = [
        jnp.where(plane[0] > j, unpacked(step.astype(F32)), 0.0).astype(BF16) for j, step in enumerate(squeezed_in)
    ]
    for cols in blocks(WIDTH, WIDE):
        x = x0[:, cols].astype(F32)
        for j, step in enumerate(steps):
            x = (x + nn(step, widths[j, :, cols])).astype(BF16).astype(F32)
        if xs is not x0:
            xs[:, cols] = x.astype(BF16)
        total = total + jnp.sum(x * x, axis=1, keepdims=True)
    inverse = lax.rsqrt(total * (1.0 / WIDTH) + EPSILON)
    lowered = jnp.zeros((TOKENS, RANK), F32)
    for cols in blocks(WIDTH, WIDE):
        value = (xs[:, cols].astype(F32) * inverse * gain[:, cols]).astype(BF16)
        normed[:, cols] = value
        lowered = lowered + nt(value, into[:, cols])
    lowered = lowered.astype(BF16)
    return inverse, lowered


def forward_tail(plane, tick, squeezed_in, lowered, normed, frozen, onto, back, out, arrived):
    squeezed = jnp.zeros((TOKENS, RANK), F32)
    for i, cols in enumerate(blocks(HIDDEN, NARROW)):
        arrived(i)
        pre = nn(normed[...], frozen[:, cols]) + nn(lowered, onto[:, cols])
        hidden = (pre * jax.nn.sigmoid(pre)).astype(BF16)
        squeezed = squeezed + nt(hidden, back[:, cols])
    squeezed = packed(squeezed)
    for j in range(tick):
        out[j] = jnp.where(plane[0] == j, squeezed, squeezed_in[j].astype(F32)).astype(BF16)
    out[tick] = jnp.where(plane[0] == tick, squeezed, 0.0).astype(BF16)


def forward_first_kernel(plane, joined, gain, weights, out, frozen, normed, sems):
    x0, into = joined.at[0:128, :], joined.at[128:192, :]
    onto, back = joined.at[192:256, 0:2048], joined.at[192:256, 2048:4096]
    moves = [
        pltpu.make_async_copy(weights.at[:, cols], frozen.at[:, cols], sems.at[i])
        for i, cols in enumerate(blocks(HIDDEN, NARROW))
    ]
    for move in moves:
        move.start()
    _, lowered = forward_body(plane, x0, [], None, gain, into, x0, normed)
    forward_tail(plane, 0, None, lowered, normed, frozen, onto, back, out, lambda i: moves[i].wait())


def forward_kernel(tick, plane, x0, squeezed_in, widths, gain, frozen, into, onto, back, out, xs, normed):
    _, lowered = forward_body(plane, x0, [squeezed_in[j] for j in range(tick)], widths, gain, into, xs, normed)
    forward_tail(plane, tick, squeezed_in, lowered, normed, frozen, onto, back, out, lambda i: None)


def transpose_kernel(first, rows, frozen, after, out):
    for r in range(0, rows, 256):
        for cols in blocks(HIDDEN, WIDE):
            out[cols, r : r + 256] = frozen[first + r : first + r + 256, cols].T


def forward_last_kernel(
    plane, x0, squeezed_in, widths, gain, frozen, into, onto, back, own_width, source, target,
    xs, normed, inverse_out, lowered_out, slope, hidden_out, squeezed_out, seed, projected,
):
    steps = [squeezed_in[j] for j in range(SECTIONS - 1)]
    inverse, lowered = forward_body(plane, x0, steps, widths, gain, into, xs, normed)
    inverse_out[...] = inverse
    lowered_out[...] = lowered
    squeezed = jnp.zeros((TOKENS, RANK), F32)
    for cols in blocks(HIDDEN, NARROW):
        pre = nn(normed[...], frozen[:, cols]) + nn(lowered, onto[:, cols])
        sigmoid = jax.nn.sigmoid(pre)
        hidden = (pre * sigmoid).astype(BF16)
        slope[:, cols] = sigmoid * (1.0 + pre * (1.0 - sigmoid))
        hidden_out[:, cols] = hidden
        squeezed = squeezed + nt(hidden, back[:, cols])
    squeezed = squeezed.astype(BF16)
    squeezed_out[...] = squeezed
    scale = 8192.0 ** (-0.5)
    total = jnp.zeros((TOKENS, RANK), F32)
    for i, cols in enumerate(blocks(WIDTH, WIDE)):
        prediction = (xs[:, cols].astype(F32) + nn(squeezed, own_width[:, cols])).astype(BF16).astype(F32)
        part = slice((i % 2) * WIDE, (i % 2) * WIDE + WIDE)
        velocity = target[:, cols].astype(F32) - source[i // 2, :, part].astype(F32)
        value = ((prediction - velocity) * scale).astype(BF16)
        seed[:, cols] = value
        total = total + nt(value, own_width[:, cols])
    projected[...] = total


def backward_body(d_squeezed, back, slope, onto, turned, into, xs, inverse, gain, d_pre, d_unit, gain_out):
    d_lowered = jnp.zeros((TOKENS, RANK), F32)
    for cols in blocks(HIDDEN, NARROW):
        value = (nn(d_squeezed, back[:, cols]) * slope[:, cols]).astype(BF16)
        d_pre[:, cols] = value
        d_lowered = d_lowered + nt(value, onto[:, cols])
    d_lowered = d_lowered.astype(BF16)
    total = jnp.zeros((TOKENS, 1), F32)
    for i, cols in enumerate(blocks(WIDTH, WIDE)):
        at = (i % 3) * WIDE
        d_normed = nn(d_pre[...], turned[i // 3][:, at : at + WIDE]) + nn(d_lowered, into[:, cols])
        unit = xs[:, cols].astype(F32) * inverse[...]
        if gain_out is not None:
            gain_out[:, cols] = jnp.sum(d_normed * unit, axis=0, keepdims=True)
        else:
            value = d_normed * gain[:, cols]
            d_unit[:, cols] = value
            total = total + jnp.sum(value * unit, axis=1, keepdims=True)
    return d_lowered, total


def backward_kernel(
    tick, plane, own, received, back, slope, onto, turned_a, turned_b, turned_c, into, xs, inverse, gain, widths,
    out, own_out, d_stream, d_pre,
):
    count = SECTIONS - 1 - tick
    if tick:
        base = [unpacked(received[j]) for j in range(count + 1)]
        own_out[...] = jnp.where(plane[0] == count, base[count], own[...])
    else:
        base = [jnp.zeros((TOKENS, RANK), F32)] * count
        own_out[...] = own[...]
    turned = (turned_a, turned_b, turned_c)
    _, total = backward_body(
        own_out[...].astype(BF16), back, slope, onto, turned, into, xs, inverse, gain, d_pre, d_stream, None
    )
    mean = total * (1.0 / WIDTH)
    sums = [base[j] for j in range(count)]
    for cols in blocks(WIDTH, WIDE):
        unit = xs[:, cols].astype(F32) * inverse[...]
        value = inverse[...] * (d_stream[:, cols] - unit * mean)
        d_stream[:, cols] = value
        if tick == 0:
            value = received[:, cols].astype(F32) + value
        narrow = value.astype(BF16)
        for j in range(count):
            sums[j] = sums[j] + nt(narrow, widths[j, :, cols])
    for j in range(count):
        out[j] = packed(sums[j])


def hand_down_kernel(tick, plane, seed, d_stream, *rest):
    out = rest[-1]
    rows = pl.ds(pl.multiple_of(jnp.clip(tick - (SECTIONS - 1 - plane[0]), 0, 1) * 64, 64), 64)
    for cols in blocks(WIDTH, WIDE):
        held = seed[rows, cols].astype(F32)
        if len(rest) == 2:
            held = jnp.where(plane[0] == SECTIONS - 1, held, rest[0][:, cols].astype(F32))
        out[:, cols] = (held + d_stream[rows, cols]).astype(BF16)


def cut(grads, core, keep, send):
    piece = grads.shape[1] // 8
    for q in range(4):
        keep[q] = grads[:, pl.ds(pl.multiple_of((core * 4 + q) * piece, 128), piece)]
        send[q] = grads[:, pl.ds(pl.multiple_of(((1 - core) * 4 + q) * piece, 128), piece)]


def backward_last_kernel(
    plane, own, received, back, slope, onto, turned_a, turned_b, turned_c, into, xs, inverse, gain, normed, lowered,
    hidden, keep, send, d_pre, gain_row, grads,
):
    d_squeezed = jnp.where(plane[0] == 0, unpacked(received[0]), own[...]).astype(BF16)
    turned = (turned_a, turned_b, turned_c)
    d_lowered, _ = backward_body(
        d_squeezed, back, slope, onto, turned, into, xs, inverse, gain, d_pre, None, gain_row
    )
    for cols in blocks(WIDTH, WIDE):
        grads[:, cols] = tn(d_lowered, normed[:, cols])
    for cols in blocks(HIDDEN, WIDE):
        grads[:, 4096 + cols.start : 4096 + cols.stop] = tn(lowered[...], d_pre[:, cols])
        grads[:, 6144 + cols.start : 6144 + cols.stop] = tn(d_squeezed, hidden[:, cols])
    grads[:, 8192:9216] = jnp.zeros((RANK, 1024), F32)
    for q in range(4):
        grads[q : q + 1, 8192:9216] = gain_row[:, q * 1024 : q * 1024 + 1024]
    cut(grads, plane[1], keep, send)


def outward_kernel(plane, squeezed, seed, first, second, third, fourth, keep, send, grads):
    index = plane[0]
    for cols in blocks(WIDTH, WIDE):
        early = jnp.where(index == 2, first[:, cols], jnp.where(index == 1, second[:, cols], third[:, cols]))
        early = jnp.where(index == 3, seed[0:64, cols], early)
        late = jnp.where(index == 3, seed[64:128, cols], fourth[:, cols])
        grads[:, cols] = tn(squeezed[0:64, :], early) + tn(squeezed[64:128, :], late)
    cut(grads, plane[1], keep, send)


def core_sum_kernel(plane, inner, inner_other, outer, outer_other, top, bottom, own, right, left):
    for k, outs in ((2, (top, bottom)), (1, (right,)), (3, (left,)), (0, (own,))):
        q = lax.rem(plane[2] + k, 4)
        for half, out in enumerate(outs):
            rows = slice(half * 32, half * 32 + 64 // len(outs))
            out[:, 0:1152] = inner[q, rows, :] + inner_other[q, rows, :]
            out[:, 1152:1664] = outer[q, rows, :] + outer_other[q, rows, :]


def add_rows_kernel(right, top, left, bottom, right_out, left_out):
    right_out[0:32, :] = right[0:32, :] + top[...]
    right_out[32:64, :] = right[32:64, :]
    left_out[0:32, :] = left[0:32, :]
    left_out[32:64, :] = left[32:64, :] + bottom[...]


def x_sum_kernel(own, first, second, out):
    out[...] = (own[...] + first[...]) + second[...]


def z_sum_kernel(parts, out):
    total = parts[0]
    for k in range(1, 8):
        total = total + parts[k]
    for k in range(8):
        out[k] = total


def outputs_kernel(plane, *refs):
    pieces, others, (gain, into, onto, back, width, inner, outer) = refs[0:5], refs[5:10], refs[10:]
    for side, group in ((plane[1], pieces), (1 - plane[1], others)):
        for k, first, piece in zip((0, 3, 1, 2, 2), (0, 0, 0, 0, 32), group):
            q = side * 4 + lax.rem(plane[2] + k, 4)
            rows = slice(first, first + piece.shape[0])
            inner[rows, pl.ds(pl.multiple_of(q * 1152, 128), 1152)] = piece[:, 0:1152]
            outer[rows, pl.ds(pl.multiple_of(q * 512, 128), 512)] = piece[:, 1152:1664]
    for q in range(4):
        gain[:, q * 1024 : q * 1024 + 1024] = inner[q : q + 1, 8192:9216]
    into[...] = inner[:, 0:4096]
    onto[...] = inner[:, 4096:6144]
    back[...] = inner[:, 6144:8192]
    width[...] = outer[...]


def exchange(x, axis):
    return lax.all_to_all(x, axis, split_axis=0, concat_axis=0, tiled=True)


def copies(x, count):
    return jnp.broadcast_to(x[None], (count,) + x.shape)


SWAP = [(0, 1), (1, 0)]


def rightward(x):
    return lax.ppermute(x, "x", [(i, (i + 1) % 4) for i in range(4)])


def leftward(x):
    return lax.ppermute(x, "x", [((i + 1) % 4, i) for i in range(4)])


def per_device(
    perturbed,
    control_token_states,
    owners,
    matched_control_row,
    cell_time_bins,
    frozen,
    section_norm_gain,
    adapter_into_rank,
    adapter_onto_hidden,
    adapter_hidden_to_rank,
    adapter_to_width,
):
    plane = lax.axis_index("pipe")
    position = lax.axis_index(DP)
    places = jnp.stack([plane, lax.axis_index("core"), lax.axis_index("x")]).astype(jnp.int32)

    weights = lax.all_gather(frozen[0], DP, axis=0, tiled=True)

    names = owners[:, :, 0]
    same = (names[:, :, None] == names[:, None, :]) & jnp.tril(jnp.ones((64, 64), bool), -1)[None]
    rank = jnp.sum(same.astype(jnp.int32), axis=2)
    batch = jnp.arange(2, dtype=jnp.int32)[:, None]
    slot = (names * 8 + batch * 4 + rank).reshape(TOKENS)
    row = (batch * 64 + matched_control_row).reshape(TOKENS)
    chosen = slot[:, None] == jnp.arange(512, dtype=jnp.int32)[None, :]
    table = jnp.sum(jnp.where(chosen, row[:, None], 0), axis=0).reshape(64, 8)
    own_width = adapter_to_width[0]
    before = [lax.ppermute(own_width, "pipe", [(i, i + k) for i in range(SECTIONS - k)]) for k in (1, 2, 3)]
    asked, *before = lax.optimization_barrier((exchange(table, DP), *before))
    asked = asked.reshape(512)

    pool = control_token_states.reshape(TOKENS, WIDTH)
    quarter = lax.dynamic_slice_in_dim(pool, plane * 1024, 1024, axis=1)
    picked = nn((asked[:, None] == jnp.arange(TOKENS, dtype=jnp.int32)[None, :]).astype(BF16), quarter)
    arrived = exchange(picked.astype(BF16).reshape(64, 8, 1024), DP).reshape(512, 1024)
    own_quarter = nn(chosen.astype(BF16), arrived).astype(BF16)
    source = exchange(copies(own_quarter, SECTIONS), "pipe")

    cell = position // 32
    bins = jnp.where(cell == 0, cell_time_bins[:, 0], cell_time_bins[:, 1])
    t_val = (bins.astype(F32) + 0.5) / NBINS
    frequency = jnp.exp(-jnp.log(10000.0) * jnp.arange(WIDTH // 2, dtype=F32) / (WIDTH // 2))
    angles = (t_val * 1000.0)[:, None] * frequency[None, :]
    features = jnp.concatenate([jnp.sin(angles), jnp.cos(angles)], axis=1)
    target = perturbed.reshape(TOKENS, WIDTH)
    gain = section_norm_gain
    into = adapter_into_rank[0].T
    onto = adapter_onto_hidden[0]
    back = adapter_hidden_to_rank[0].T
    x0, joined = call(
        entry_kernel,
        [((TOKENS, WIDTH), BF16), ((2 * TOKENS, WIDTH), BF16)],
        [t_val, source, target, features, into, onto, back],
        smem=1,
    )
    stream = ((TOKENS, WIDTH), BF16)
    down = [(i, (i + 1) % SECTIONS) for i in range(SECTIONS)]
    up = [((i + 1) % SECTIONS, i) for i in range(SECTIONS)]

    (widths,) = call(widths_kernel, [((SECTIONS, RANK, WIDTH), BF16)], [places, own_width, *before], smem=1)
    (squeezed_out,) = call(
        forward_first_kernel,
        [((1, 64, 128), BF16)],
        [places, joined, gain, weights],
        scratch=[((WIDTH, HIDDEN), BF16), stream, pltpu.SemaphoreType.DMA((8,))],
        smem=1,
        hbm=(3,),
        limit=36,
        cost=6,
    )
    turned = []
    for tick in range(1, SECTIONS):
        squeezed_in = lax.ppermute(squeezed_out, "pipe", down)
        rows = PARTS[tick - 1]
        turned += call(
            functools.partial(transpose_kernel, sum(PARTS[: tick - 1]), rows),
            [((HIDDEN, rows), BF16)],
            [weights, squeezed_out],
            cost=3,
        )
        squeezed_in, turned[-1] = lax.optimization_barrier((squeezed_in, turned[-1]))
        if tick < SECTIONS - 1:
            (squeezed_out,) = call(
                functools.partial(forward_kernel, tick),
                [((tick + 1, 64, 128), BF16)],
                [places, x0, squeezed_in, widths, gain, weights, into, onto, back],
                scratch=[stream, stream],
                smem=1,
                cost=6,
            )
    xs, normed, inverse, lowered, slope, hidden, squeezed, seed, projected = call(
        forward_last_kernel,
        [
            stream,
            stream,
            ((TOKENS, 1), F32),
            ((TOKENS, RANK), BF16),
            ((TOKENS, HIDDEN), F32),
            ((TOKENS, HIDDEN), BF16),
            ((TOKENS, RANK), BF16),
            stream,
            ((TOKENS, RANK), F32),
        ],
        [places, x0, squeezed_in, widths, gain, weights, into, onto, back, own_width, source, target],
        smem=1,
        limit=5,
        cost=8,
    )

    own, received = projected, seed
    arrivals = []

    def hand_down(tick, d_stream, arrived):
        (handed,) = call(
            functools.partial(hand_down_kernel, tick),
            [((64, WIDTH), BF16)],
            [places, seed, d_stream, *arrivals[-1:]],
            smem=1,
        )
        handed, arrived = lax.optimization_barrier((handed, arrived))
        arrivals.append(lax.ppermute(handed, "pipe", up))
        return arrived

    for tick in range(SECTIONS - 1):
        sent, own, d_stream = call(
            functools.partial(backward_kernel, tick),
            [((SECTIONS - 1 - tick, 64, 128), F32), ((TOKENS, RANK), F32), ((TOKENS, WIDTH), F32)],
            [places, own, received, back, slope, onto, *turned, into, xs, inverse, gain, widths],
            scratch=[((TOKENS, HIDDEN), BF16)],
            smem=1,
            cost=8,
        )
        received = hand_down(tick, d_stream, lax.ppermute(sent, "pipe", up))
    keep, send = call(
        backward_last_kernel,
        [((4, RANK, 1152), F32)] * 2,
        [places, own, received, back, slope, onto, *turned, into, xs, inverse, gain, normed, lowered, hidden],
        scratch=[((TOKENS, HIDDEN), BF16), ((1, WIDTH), F32), ((RANK, 9216), F32)],
        smem=1,
        cost=8,
    )
    arrivals[-1], keep = lax.optimization_barrier((arrivals[-1], keep))
    hand_down(SECTIONS - 1, d_stream, received)
    inner = [keep, lax.ppermute(send, "core", SWAP)]
    keep, send = call(
        outward_kernel,
        [((4, RANK, 512), F32)] * 2,
        [places, squeezed, seed, *arrivals],
        scratch=[((RANK, WIDTH), F32)],
        smem=1,
    )
    piece, part = ((RANK, 1664), F32), ((RANK // 2, 1664), F32)
    top, bottom, own_piece, right, left = call(
        core_sum_kernel,
        [part, part, piece, piece, piece],
        [places, *inner, keep, lax.ppermute(send, "core", SWAP)],
        smem=1,
    )
    right, left = call(add_rows_kernel, [piece, piece], [right, rightward(top), left, leftward(bottom)])
    (along_x,) = call(x_sum_kernel, [piece], [own_piece, rightward(right), leftward(left)])
    (along_z,) = call(z_sum_kernel, [((8, 8, 1664), F32)], [exchange(along_x.reshape(8, 8, 1664), "z")])
    rows = exchange(along_z, "z").reshape(RANK, 1664)
    before, after = rightward(rows), leftward(rows)
    pieces = [rows, before, after, rightward(before[0:32]), leftward(after[32:64])]
    others = [lax.ppermute(p, "core", SWAP) for p in pieces]
    g_gain, g_into, g_onto, g_back, g_width = call(
        outputs_kernel,
        [((1, WIDTH), F32), ((RANK, WIDTH), F32), ((RANK, HIDDEN), F32), ((RANK, HIDDEN), F32), ((RANK, WIDTH), F32)],
        [places, *pieces, *others],
        scratch=[((RANK, 9216), F32), ((RANK, WIDTH), F32)],
        smem=1,
    )
    return g_gain, g_into.T[None], g_onto[None], g_back.T[None], g_width[None]


def solution(mesh):
    cells = Mesh(mesh.devices.reshape(8, 4, 2, 4), ("z", "x", "core", "pipe"))
    in_specs = (
        P(None, DP, None),
        P(None, DP, None),
        P(None, DP, None),
        P(None, DP),
        P(),
        P("pipe", DP, None),
        P("pipe", None),
        P("pipe", None, None),
        P("pipe", None, None),
        P("pipe", None, None),
        P("pipe", None, None),
    )
    out_specs = (
        P("pipe", None),
        P("pipe", None, None),
        P("pipe", None, None),
        P("pipe", None, None),
        P("pipe", None, None),
    )
    return jax.shard_map(per_device, mesh=cells, in_specs=in_specs, out_specs=out_specs, check_vma=False)
```

```python
import functools

import jax
import jax.numpy as jnp
from jax import lax
from jax.experimental import pallas as pl
from jax.experimental.pallas import tpu as pltpu
from jax.sharding import Mesh
from jax.sharding import PartitionSpec as P

NBINS = 1000
EPSILON = 1e-05
TOKENS = 128
WIDTH = 4096
HIDDEN = 2048
RANK = 64
SECTIONS = 4
WIDE = 512
NARROW = 256
DP = ("z", "x", "core")
F32 = jnp.float32
BF16 = jnp.bfloat16
VMEM = pl.BlockSpec(memory_space=pltpu.VMEM)
SMEM = pl.BlockSpec(memory_space=pltpu.SMEM)
HBM = pl.BlockSpec(memory_space=pltpu.HBM)
PARTS = (1536, 1536, 1024)


def nn(left, right):
    return jnp.dot(left, right, preferred_element_type=F32)


def nt(left, right):
    return lax.dot_general(left, right, (((1,), (1,)), ((), ())), preferred_element_type=F32)


def tn(left, right):
    return lax.dot_general(left, right, (((0,), (0,)), ((), ())), preferred_element_type=F32)


def packed(value):
    return jnp.concatenate([value[0:64], value[64:128]], axis=1)


def unpacked(value):
    return jnp.concatenate([value[:, 0:64], value[:, 64:128]], axis=0)


def call(kernel, outs, args, scratch=(), smem=0, hbm=(), limit=8, cost=1):
    specs = [SMEM if i < smem else HBM if i in hbm else VMEM for i in range(len(args))]
    out_shape = tuple(jax.ShapeDtypeStruct(s, d) for s, d in outs)
    return pl.pallas_call(
        kernel,
        in_specs=specs,
        out_specs=tuple(VMEM for _ in outs),
        out_shape=out_shape,
        scratch_shapes=[s if hasattr(s, "memory_space") else pltpu.VMEM(*s) for s in scratch],
        cost_estimate=pl.CostEstimate(
            flops=cost * 10**9, bytes_accessed=cost * 3 * 10**6, transcendentals=0
        ),
        compiler_params=pltpu.CompilerParams(vmem_limit_bytes=limit << 20),
    )(*args)


def blocks(total, size):
    return [slice(i, i + size) for i in range(0, total, size)]


def entry_kernel(time_ref, source_ref, target_ref, feature_ref, into, onto, back, out_ref, joined):
    for batch in range(2):
        rows = slice(batch * 64, batch * 64 + 64)
        t = time_ref[batch]
        for q in range(SECTIONS):
            cols = slice(q * 1024, q * 1024 + 1024)
            source = source_ref[q, rows, :].astype(F32)
            target = target_ref[rows, cols].astype(F32)
            feature = feature_ref[batch : batch + 1, cols]
            value = ((1.0 - t) * source + t * target + feature).astype(BF16)
            out_ref[rows, cols] = value
            joined[rows, cols] = value
    joined[128:192, :] = into[...]
    joined[192:256, 0:2048] = onto[...]
    joined[192:256, 2048:4096] = back[...]


def widths_kernel(plane, own, one, two, three, out):
    for j in range(SECTIONS):
        for cols in blocks(WIDTH, WIDE):
            value = jnp.where(plane[0] == j, own[:, cols].astype(F32), 0.0)
            for k, part in ((1, one), (2, two), (3, three)):
                value = jnp.where(plane[0] == j + k, part[:, cols].astype(F32), value)
            out[j, :, cols] = value.astype(BF16)


def forward_body(plane, x0, squeezed_in, widths, gain, into, xs, normed):
    total = jnp.zeros((TOKENS, 1), F32)
    steps = [
        jnp.where(plane[0] > j, unpacked(step.astype(F32)), 0.0).astype(BF16) for j, step in enumerate(squeezed_in)
    ]
    for cols in blocks(WIDTH, WIDE):
        x = x0[:, cols].astype(F32)
        for j, step in enumerate(steps):
            x = (x + nn(step, widths[j, :, cols])).astype(BF16).astype(F32)
        if xs is not x0:
            xs[:, cols] = x.astype(BF16)
        total = total + jnp.sum(x * x, axis=1, keepdims=True)
    inverse = lax.rsqrt(total * (1.0 / WIDTH) + EPSILON)
    lowered = jnp.zeros((TOKENS, RANK), F32)
    for cols in blocks(WIDTH, WIDE):
        value = (xs[:, cols].astype(F32) * inverse * gain[:, cols]).astype(BF16)
        normed[:, cols] = value
        lowered = lowered + nt(value, into[:, cols])
    lowered = lowered.astype(BF16)
    return inverse, lowered


def forward_tail(plane, tick, squeezed_in, lowered, normed, frozen, onto, back, out, arrived):
    squeezed = jnp.zeros((TOKENS, RANK), F32)
    for i, cols in enumerate(blocks(HIDDEN, NARROW)):
        arrived(i)
        pre = nn(normed[...], frozen[:, cols]) + nn(lowered, onto[:, cols])
        hidden = (pre * jax.nn.sigmoid(pre)).astype(BF16)
        squeezed = squeezed + nt(hidden, back[:, cols])
    squeezed = packed(squeezed)
    for j in range(tick):
        out[j] = jnp.where(plane[0] == j, squeezed, squeezed_in[j].astype(F32)).astype(BF16)
    out[tick] = jnp.where(plane[0] == tick, squeezed, 0.0).astype(BF16)


def forward_first_kernel(plane, joined, gain, weights, out, frozen, normed, sems):
    x0, into = joined.at[0:128, :], joined.at[128:192, :]
    onto, back = joined.at[192:256, 0:2048], joined.at[192:256, 2048:4096]
    moves = [
        pltpu.make_async_copy(weights.at[:, cols], frozen.at[:, cols], sems.at[i])
        for i, cols in enumerate(blocks(HIDDEN, NARROW))
    ]
    for move in moves:
        move.start()
    _, lowered = forward_body(plane, x0, [], None, gain, into, x0, normed)
    forward_tail(plane, 0, None, lowered, normed, frozen, onto, back, out, lambda i: moves[i].wait())


def forward_kernel(tick, plane, x0, squeezed_in, widths, gain, frozen, into, onto, back, out, xs, normed):
    _, lowered = forward_body(plane, x0, [squeezed_in[j] for j in range(tick)], widths, gain, into, xs, normed)
    forward_tail(plane, tick, squeezed_in, lowered, normed, frozen, onto, back, out, lambda i: None)


def transpose_kernel(first, rows, frozen, after, out):
    for r in range(0, rows, 256):
        for cols in blocks(HIDDEN, WIDE):
            out[cols, r : r + 256] = frozen[first + r : first + r + 256, cols].T


def forward_last_kernel(
    plane, x0, squeezed_in, widths, gain, frozen, into, onto, back, own_width, source, target,
    xs, normed, inverse_out, lowered_out, slope, hidden_out, squeezed_out, seed, projected,
):
    steps = [squeezed_in[j] for j in range(SECTIONS - 1)]
    inverse, lowered = forward_body(plane, x0, steps, widths, gain, into, xs, normed)
    inverse_out[...] = inverse
    lowered_out[...] = lowered
    squeezed = jnp.zeros((TOKENS, RANK), F32)
    for cols in blocks(HIDDEN, NARROW):
        pre = nn(normed[...], frozen[:, cols]) + nn(lowered, onto[:, cols])
        sigmoid = jax.nn.sigmoid(pre)
        hidden = (pre * sigmoid).astype(BF16)
        slope[:, cols] = sigmoid * (1.0 + pre * (1.0 - sigmoid))
        hidden_out[:, cols] = hidden
        squeezed = squeezed + nt(hidden, back[:, cols])
    squeezed = squeezed.astype(BF16)
    squeezed_out[...] = squeezed
    scale = 8192.0 ** (-0.5)
    total = jnp.zeros((TOKENS, RANK), F32)
    for i, cols in enumerate(blocks(WIDTH, WIDE)):
        prediction = (xs[:, cols].astype(F32) + nn(squeezed, own_width[:, cols])).astype(BF16).astype(F32)
        part = slice((i % 2) * WIDE, (i % 2) * WIDE + WIDE)
        velocity = target[:, cols].astype(F32) - source[i // 2, :, part].astype(F32)
        value = ((prediction - velocity) * scale).astype(BF16)
        seed[:, cols] = value
        total = total + nt(value, own_width[:, cols])
    projected[...] = total


def backward_body(d_squeezed, back, slope, onto, turned, into, xs, inverse, gain, d_pre, d_unit, gain_out):
    d_lowered = jnp.zeros((TOKENS, RANK), F32)
    for cols in blocks(HIDDEN, NARROW):
        value = (nn(d_squeezed, back[:, cols]) * slope[:, cols]).astype(BF16)
        d_pre[:, cols] = value
        d_lowered = d_lowered + nt(value, onto[:, cols])
    d_lowered = d_lowered.astype(BF16)
    total = jnp.zeros((TOKENS, 1), F32)
    for i, cols in enumerate(blocks(WIDTH, WIDE)):
        at = (i % 3) * WIDE
        d_normed = nn(d_pre[...], turned[i // 3][:, at : at + WIDE]) + nn(d_lowered, into[:, cols])
        unit = xs[:, cols].astype(F32) * inverse[...]
        if gain_out is not None:
            gain_out[:, cols] = jnp.sum(d_normed * unit, axis=0, keepdims=True)
        else:
            value = d_normed * gain[:, cols]
            d_unit[:, cols] = value
            total = total + jnp.sum(value * unit, axis=1, keepdims=True)
    return d_lowered, total


def backward_kernel(
    tick, plane, own, received, back, slope, onto, turned_a, turned_b, turned_c, into, xs, inverse, gain, widths,
    out, own_out, d_stream, d_pre,
):
    count = SECTIONS - 1 - tick
    if tick:
        base = [unpacked(received[j]) for j in range(count + 1)]
        own_out[...] = jnp.where(plane[0] == count, base[count], own[...])
    else:
        base = [jnp.zeros((TOKENS, RANK), F32)] * count
        own_out[...] = own[...]
    turned = (turned_a, turned_b, turned_c)
    _, total = backward_body(
        own_out[...].astype(BF16), back, slope, onto, turned, into, xs, inverse, gain, d_pre, d_stream, None
    )
    mean = total * (1.0 / WIDTH)
    sums = [base[j] for j in range(count)]
    for cols in blocks(WIDTH, WIDE):
        unit = xs[:, cols].astype(F32) * inverse[...]
        value = inverse[...] * (d_stream[:, cols] - unit * mean)
        d_stream[:, cols] = value
        if tick == 0:
            value = received[:, cols].astype(F32) + value
        narrow = value.astype(BF16)
        for j in range(count):
            sums[j] = sums[j] + nt(narrow, widths[j, :, cols])
    for j in range(count):
        out[j] = packed(sums[j])


def hand_down_kernel(tick, plane, seed, d_stream, *rest):
    out = rest[-1]
    rows = pl.ds(pl.multiple_of(jnp.clip(tick - (SECTIONS - 1 - plane[0]), 0, 1) * 64, 64), 64)
    for cols in blocks(WIDTH, WIDE):
        held = seed[rows, cols].astype(F32)
        if len(rest) == 2:
            held = jnp.where(plane[0] == SECTIONS - 1, held, rest[0][:, cols].astype(F32))
        out[:, cols] = (held + d_stream[rows, cols]).astype(BF16)


def cut(grads, core, keep, send):
    piece = grads.shape[1] // 8
    for q in range(4):
        keep[q] = grads[:, pl.ds(pl.multiple_of((core * 4 + q) * piece, 128), piece)]
        send[q] = grads[:, pl.ds(pl.multiple_of(((1 - core) * 4 + q) * piece, 128), piece)]


def backward_last_kernel(
    plane, own, received, back, slope, onto, turned_a, turned_b, turned_c, into, xs, inverse, gain, normed, lowered,
    hidden, keep, send, d_pre, gain_row, grads,
):
    d_squeezed = jnp.where(plane[0] == 0, unpacked(received[0]), own[...]).astype(BF16)
    turned = (turned_a, turned_b, turned_c)
    d_lowered, _ = backward_body(
        d_squeezed, back, slope, onto, turned, into, xs, inverse, gain, d_pre, None, gain_row
    )
    for cols in blocks(WIDTH, WIDE):
        grads[:, cols] = tn(d_lowered, normed[:, cols])
    for cols in blocks(HIDDEN, WIDE):
        grads[:, 4096 + cols.start : 4096 + cols.stop] = tn(lowered[...], d_pre[:, cols])
        grads[:, 6144 + cols.start : 6144 + cols.stop] = tn(d_squeezed, hidden[:, cols])
    grads[:, 8192:9216] = jnp.zeros((RANK, 1024), F32)
    for q in range(4):
        grads[q : q + 1, 8192:9216] = gain_row[:, q * 1024 : q * 1024 + 1024]
    cut(grads, plane[1], keep, send)


def outward_kernel(plane, squeezed, seed, first, second, third, fourth, keep, send, grads):
    index = plane[0]
    for cols in blocks(WIDTH, WIDE):
        early = jnp.where(index == 2, first[:, cols], jnp.where(index == 1, second[:, cols], third[:, cols]))
        early = jnp.where(index == 3, seed[0:64, cols], early)
        late = jnp.where(index == 3, seed[64:128, cols], fourth[:, cols])
        grads[:, cols] = tn(squeezed[0:64, :], early) + tn(squeezed[64:128, :], late)
    cut(grads, plane[1], keep, send)


def core_sum_kernel(plane, keep, other, top, bottom, own, right, left):
    for k, outs in ((2, (top, bottom)), (1, (right,)), (3, (left,)), (0, (own,))):
        q = lax.rem(plane[2] + k, 4)
        for half, out in enumerate(outs):
            rows = slice(half * 32, half * 32 + 64 // len(outs))
            out[...] = keep[q, rows, :] + other[q, rows, :]


def add_rows_kernel(right, top, left, bottom, right_out, left_out):
    right_out[0:32, :] = right[0:32, :] + top[...]
    right_out[32:64, :] = right[32:64, :]
    left_out[0:32, :] = left[0:32, :]
    left_out[32:64, :] = left[32:64, :] + bottom[...]


def x_sum_kernel(inner, inner_first, inner_second, outer, outer_first, outer_second, out):
    out[:, 0:1152] = (inner[...] + inner_first[...]) + inner_second[...]
    out[:, 1152:1664] = (outer[...] + outer_first[...]) + outer_second[...]


def z_sum_kernel(parts, out):
    total = parts[0]
    for k in range(1, 8):
        total = total + parts[k]
    for k in range(8):
        out[k] = total


def outputs_kernel(plane, *refs):
    pieces, others, (gain, into, onto, back, width, inner, outer) = refs[0:5], refs[5:10], refs[10:]
    for side, group in ((plane[1], pieces), (1 - plane[1], others)):
        for k, first, piece in zip((0, 3, 1, 2, 2), (0, 0, 0, 0, 32), group):
            q = side * 4 + lax.rem(plane[2] + k, 4)
            rows = slice(first, first + piece.shape[0])
            inner[rows, pl.ds(pl.multiple_of(q * 1152, 128), 1152)] = piece[:, 0:1152]
            outer[rows, pl.ds(pl.multiple_of(q * 512, 128), 512)] = piece[:, 1152:1664]
    for q in range(4):
        gain[:, q * 1024 : q * 1024 + 1024] = inner[q : q + 1, 8192:9216]
    into[...] = inner[:, 0:4096]
    onto[...] = inner[:, 4096:6144]
    back[...] = inner[:, 6144:8192]
    width[...] = outer[...]


def exchange(x, axis):
    return lax.all_to_all(x, axis, split_axis=0, concat_axis=0, tiled=True)


def copies(x, count):
    return jnp.broadcast_to(x[None], (count,) + x.shape)


SWAP = [(0, 1), (1, 0)]


def rightward(x):
    return lax.ppermute(x, "x", [(i, (i + 1) % 4) for i in range(4)])


def leftward(x):
    return lax.ppermute(x, "x", [((i + 1) % 4, i) for i in range(4)])


def ring_start(places, keep, send):
    piece, part = ((RANK, keep.shape[2]), F32), ((RANK // 2, keep.shape[2]), F32)
    top, bottom, own, right, left = call(
        core_sum_kernel, [part, part, piece, piece, piece], [places, keep, lax.ppermute(send, "core", SWAP)], smem=1
    )
    return [right, rightward(top), left, leftward(bottom), own]


def ring_end(parts):
    own = parts[-1]
    right, left = call(add_rows_kernel, [(own.shape, F32)] * 2, parts[:-1])
    return [own, rightward(right), leftward(left)]


def per_device(
    perturbed,
    control_token_states,
    owners,
    matched_control_row,
    cell_time_bins,
    frozen,
    section_norm_gain,
    adapter_into_rank,
    adapter_onto_hidden,
    adapter_hidden_to_rank,
    adapter_to_width,
):
    plane = lax.axis_index("pipe")
    position = lax.axis_index(DP)
    places = jnp.stack([plane, lax.axis_index("core"), lax.axis_index("x")]).astype(jnp.int32)

    weights = lax.all_gather(frozen[0], DP, axis=0, tiled=True)

    names = owners[:, :, 0]
    same = (names[:, :, None] == names[:, None, :]) & jnp.tril(jnp.ones((64, 64), bool), -1)[None]
    rank = jnp.sum(same.astype(jnp.int32), axis=2)
    batch = jnp.arange(2, dtype=jnp.int32)[:, None]
    slot = (names * 8 + batch * 4 + rank).reshape(TOKENS)
    row = (batch * 64 + matched_control_row).reshape(TOKENS)
    chosen = slot[:, None] == jnp.arange(512, dtype=jnp.int32)[None, :]
    table = jnp.sum(jnp.where(chosen, row[:, None], 0), axis=0).reshape(64, 8)
    own_width = adapter_to_width[0]
    before = [lax.ppermute(own_width, "pipe", [(i, i + k) for i in range(SECTIONS - k)]) for k in (1, 2, 3)]
    asked, *before = lax.optimization_barrier((exchange(table, DP), *before))
    asked = asked.reshape(512)

    pool = control_token_states.reshape(TOKENS, WIDTH)
    quarter = lax.dynamic_slice_in_dim(pool, plane * 1024, 1024, axis=1)
    picked = nn((asked[:, None] == jnp.arange(TOKENS, dtype=jnp.int32)[None, :]).astype(BF16), quarter)
    arrived = exchange(picked.astype(BF16).reshape(64, 8, 1024), DP).reshape(512, 1024)
    own_quarter = nn(chosen.astype(BF16), arrived).astype(BF16)
    source = exchange(copies(own_quarter, SECTIONS), "pipe")

    cell = position // 32
    bins = jnp.where(cell == 0, cell_time_bins[:, 0], cell_time_bins[:, 1])
    t_val = (bins.astype(F32) + 0.5) / NBINS
    frequency = jnp.exp(-jnp.log(10000.0) * jnp.arange(WIDTH // 2, dtype=F32) / (WIDTH // 2))
    angles = (t_val * 1000.0)[:, None] * frequency[None, :]
    features = jnp.concatenate([jnp.sin(angles), jnp.cos(angles)], axis=1)
    target = perturbed.reshape(TOKENS, WIDTH)
    gain = section_norm_gain
    into = adapter_into_rank[0].T
    onto = adapter_onto_hidden[0]
    back = adapter_hidden_to_rank[0].T
    x0, joined = call(
        entry_kernel,
        [((TOKENS, WIDTH), BF16), ((2 * TOKENS, WIDTH), BF16)],
        [t_val, source, target, features, into, onto, back],
        smem=1,
    )
    stream = ((TOKENS, WIDTH), BF16)
    down = [(i, (i + 1) % SECTIONS) for i in range(SECTIONS)]
    up = [((i + 1) % SECTIONS, i) for i in range(SECTIONS)]

    (widths,) = call(widths_kernel, [((SECTIONS, RANK, WIDTH), BF16)], [places, own_width, *before], smem=1)
    (squeezed_out,) = call(
        forward_first_kernel,
        [((1, 64, 128), BF16)],
        [places, joined, gain, weights],
        scratch=[((WIDTH, HIDDEN), BF16), stream, pltpu.SemaphoreType.DMA((8,))],
        smem=1,
        hbm=(3,),
        limit=36,
        cost=6,
    )
    turned = []
    for tick in range(1, SECTIONS):
        squeezed_in = lax.ppermute(squeezed_out, "pipe", down)
        rows = PARTS[tick - 1]
        turned += call(
            functools.partial(transpose_kernel, sum(PARTS[: tick - 1]), rows),
            [((HIDDEN, rows), BF16)],
            [weights, squeezed_out],
            cost=3,
        )
        squeezed_in, turned[-1] = lax.optimization_barrier((squeezed_in, turned[-1]))
        if tick < SECTIONS - 1:
            (squeezed_out,) = call(
                functools.partial(forward_kernel, tick),
                [((tick + 1, 64, 128), BF16)],
                [places, x0, squeezed_in, widths, gain, weights, into, onto, back],
                scratch=[stream, stream],
                smem=1,
                cost=6,
            )
    xs, normed, inverse, lowered, slope, hidden, squeezed, seed, projected = call(
        forward_last_kernel,
        [
            stream,
            stream,
            ((TOKENS, 1), F32),
            ((TOKENS, RANK), BF16),
            ((TOKENS, HIDDEN), F32),
            ((TOKENS, HIDDEN), BF16),
            ((TOKENS, RANK), BF16),
            stream,
            ((TOKENS, RANK), F32),
        ],
        [places, x0, squeezed_in, widths, gain, weights, into, onto, back, own_width, source, target],
        smem=1,
        limit=5,
        cost=8,
    )

    own, received = projected, seed
    arrivals = []

    def hand_down(tick, d_stream, arrived):
        (handed,) = call(
            functools.partial(hand_down_kernel, tick),
            [((64, WIDTH), BF16)],
            [places, seed, d_stream, *arrivals[-1:]],
            smem=1,
            cost=12,
        )
        handed, arrived = lax.optimization_barrier((handed, arrived))
        arrivals.append(lax.ppermute(handed, "pipe", up))
        return arrived

    for tick in range(SECTIONS - 1):
        sent, own, d_stream = call(
            functools.partial(backward_kernel, tick),
            [((SECTIONS - 1 - tick, 64, 128), F32), ((TOKENS, RANK), F32), ((TOKENS, WIDTH), F32)],
            [places, own, received, back, slope, onto, *turned, into, xs, inverse, gain, widths],
            scratch=[((TOKENS, HIDDEN), BF16)],
            smem=1,
            cost=8,
        )
        received = hand_down(tick, d_stream, lax.ppermute(sent, "pipe", up))
    keep, send = call(
        backward_last_kernel,
        [((4, RANK, 1152), F32)] * 2,
        [places, own, received, back, slope, onto, *turned, into, xs, inverse, gain, normed, lowered, hidden],
        scratch=[((TOKENS, HIDDEN), BF16), ((1, WIDTH), F32), ((RANK, 9216), F32)],
        smem=1,
        cost=1,
    )
    arrivals[-1], keep = lax.optimization_barrier((arrivals[-1], keep))
    hand_down(SECTIONS - 1, d_stream, received)
    inner = ring_start(places, keep, send)
    arrivals[-1], inner[1], inner[3] = lax.optimization_barrier((arrivals[-1], inner[1], inner[3]))
    inner = ring_end(inner)
    keep, send = call(
        outward_kernel,
        [((4, RANK, 512), F32)] * 2,
        [places, squeezed, seed, *arrivals],
        scratch=[((RANK, WIDTH), F32)],
        smem=1,
    )
    outer = ring_end(ring_start(places, keep, send))
    (along_x,) = call(x_sum_kernel, [((RANK, 1664), F32)], [*inner, *outer])
    (along_z,) = call(z_sum_kernel, [((8, 8, 1664), F32)], [exchange(along_x.reshape(8, 8, 1664), "z")])
    rows = exchange(along_z, "z").reshape(RANK, 1664)
    before, after = rightward(rows), leftward(rows)
    pieces = [rows, before, after, rightward(before[0:32]), leftward(after[32:64])]
    others = [lax.ppermute(p, "core", SWAP) for p in pieces]
    g_gain, g_into, g_onto, g_back, g_width = call(
        outputs_kernel,
        [((1, WIDTH), F32), ((RANK, WIDTH), F32), ((RANK, HIDDEN), F32), ((RANK, HIDDEN), F32), ((RANK, WIDTH), F32)],
        [places, *pieces, *others],
        scratch=[((RANK, 9216), F32), ((RANK, WIDTH), F32)],
        smem=1,
    )
    return g_gain, g_into.T[None], g_onto[None], g_back.T[None], g_width[None]


def solution(mesh):
    cells = Mesh(mesh.devices.reshape(8, 4, 2, 4), ("z", "x", "core", "pipe"))
    in_specs = (
        P(None, DP, None),
        P(None, DP, None),
        P(None, DP, None),
        P(None, DP),
        P(),
        P("pipe", DP, None),
        P("pipe", None),
        P("pipe", None, None),
        P("pipe", None, None),
        P("pipe", None, None),
        P("pipe", None, None),
    )
    out_specs = (
        P("pipe", None),
        P("pipe", None, None),
        P("pipe", None, None),
        P("pipe", None, None),
        P("pipe", None, None),
    )
    return jax.shard_map(per_device, mesh=cells, in_specs=in_specs, out_specs=out_specs, check_vma=False)
```
